128 devices in a mesh: dp: 16 (over x_lo, y, core), ctx: 8 (over z, x_hi).
Axes of the slice: x: 4 (x_hi: 2, x_lo: 2; x = x_hi * 2 + x_lo), y: 4, z: 4, core: 2. Of those that a mesh axis runs over, the one named last changes fastest.
Arguments:
- hidden_in: bfloat16 [16384, 2048], P(('dp', 'ctx')), may hold values from -4 to 4
- queries: bfloat16 [16384, 4096], P(('dp', 'ctx')), may hold values from -30 to 30
- keys: bfloat16 [16384, 512], P(('dp', 'ctx')), may hold values from -5 to 5
- values: bfloat16 [16384, 512], P(('dp', 'ctx')), may hold values from -8 to 8
- out_weight: bfloat16 [4096, 2048], P('ctx'), may hold values from -0.09375 to 0.09375
- norm_gain: float32 [2048], replicated, may hold values from 0.5 to 1.5
- routes: int32 [16384, 8], P(('dp', 'ctx')), may hold values from 0 to 127, all different within a row; in each aligned block of 128 rows (0 to 127, 128 to 255, ...) at most 12 rows name the same one
- gates: float32 [16384, 8], P(('dp', 'ctx')), may hold values from 0.05 to 0.75
- w_gate: bfloat16 [128, 2048, 768], P(('dp', 'ctx')), may hold values from -0.125 to 0.125
- w_up: bfloat16 [128, 2048, 768], P(('dp', 'ctx')), may hold values from -0.125 to 0.125
- w_down: bfloat16 [128, 768, 2048], P(('dp', 'ctx')), may hold values from -0.21875 to 0.21875
Outputs:
- attended: bfloat16 [16384, 2048], P(('dp', 'ctx'))
- expert_mix: bfloat16 [16384, 2048], P(('dp', 'ctx'))
- balance_loss: float32 [], replicated
- expert_load: float32 [128], replicated
The draws below stay inside these ranges and needn't reach their ends.
Inputs may be any that keep to these rules, and one draw needn't show every extreme that they name: `routes`: in the rows of one device no expert is named more than 12 times; some expert is named exactly 12 times.
All inputs are finite; a program needn't handle non-finite values.
Results may differ from the reference program's by a relative error of at most 0.01.
Values may be sent and summed in bfloat16 or wider, within the bound.
No kernel may reach another device: no remote copies, remote signals or barrier semaphores. Data moves between devices by JAX's collectives and lax.ppermute only.
A program may use at most 128 MiB of HBM per device.

```python
import math
import jax
import jax.numpy as jnp
import numpy as np
from jax import lax

D = 2048
H = 32
KV = 4
DH = 128
FF = 768
TOP = 8
TOK_DEV = 128
EXPERTS = 128
SEQ = 1024
TOKENS = 16384
CAP = 12
N_DP = 16
N_CTX = 8


def draw_keys(key, part):
    key = jax.random.fold_in(key, 11)
    base = 1.4 * jax.random.truncated_normal(key, -3.0, 3.0, (TOKENS, KV * DH), jnp.float32)
    return base.astype(jnp.bfloat16)


def draw_queries(key, part):
    key = jax.random.fold_in(key, 13)
    base = 1.4 * jax.random.truncated_normal(key, -3.0, 3.0, (TOKENS, H * DH), jnp.float32)
    return base.astype(jnp.bfloat16)


def draw_gates(key, part):
    key = jax.random.fold_in(key, 17)
    rows = jnp.arange(TOKENS, dtype=jnp.int32)[:, None].astype(jnp.float32)
    ramp = jnp.exp(math.log(12.0) * rows / (TOKENS - 1))
    picks = jax.random.uniform(key, (TOKENS, TOP), jnp.float32, 0.05, 0.0625)
    return jnp.clip(picks * ramp, 0.05, 0.75)


def steps_of(rng, dims, pieces, low, largest):
    def one(axis_at, shards_of):
        draws = jax.random.uniform(jax.random.fold_in(jax.random.fold_in(rng, 6), axis_at), (shards_of,), jnp.float32, low / len(pieces), largest / len(pieces))
        return jnp.repeat(jnp.exp(draws), dims[axis_at] // shards_of).reshape((-1,) + (1,) * (len(dims) - axis_at - 1))

    level = one(*pieces[0])
    for cut in pieces[1:]:
        level = level * one(*cut)
    return level


def assign_block(rng, own, number, rows, number_of, top, reach, slope):
    order = jax.random.permutation(rng, number_of)
    crowded, common = portions_of(number_of, rows * top, reach, slope, True), portions_of(number_of, rows * top, reach, slope, False)
    places = jnp.arange(number_of)

    def named(sizes, rotation):
        used = int((sizes > 0).sum())
        fixed = max(1, used // 4)
        shifted = fixed + (places - fixed + rotation * (used - fixed)) % max(1, number_of - fixed)
        return jnp.zeros((number_of,), jnp.int32).at[order[jnp.where(places < fixed, places, shifted)]].set(jnp.asarray(sizes, jnp.int32))

    sizes = jnp.where(number % 4 == 0, named(crowded, number // 4), named(common, number - number // 4 - 1))
    mixed = jax.random.permutation(jax.random.fold_in(own, 3), number_of)
    giver, sink = mixed[0:number_of // 2 * 2:2], mixed[1:number_of // 2 * 2:2]
    slack = jnp.minimum(sizes[giver] - 1, reach - sizes[sink]) // 2
    slack = jnp.where((giver == order[0]) | (sink == order[0]) | (sizes[sink] == 0), 0, jnp.maximum(slack, 0))
    shifted = jax.random.randint(jax.random.fold_in(own, 4), (number_of // 2,), 0, 1 << 20) % (slack + 1)
    sizes = sizes.at[giver].add(-shifted).at[sink].add(shifted)
    members = jnp.searchsorted(jnp.cumsum(sizes), jnp.arange(rows * top), side="right").astype(jnp.int32)
    grid = members.reshape(top, rows).T
    grid = grid[jax.random.permutation(jax.random.fold_in(own, 1), rows)]
    rotation = jax.random.randint(jax.random.fold_in(own, 2), (rows, 1), 0, top)
    return jnp.take_along_axis(grid, (jnp.arange(top)[None, :] + rotation) % top, axis=1)


def portions_of(number_of, total, limit, lean, full):
    loads = [(1 << 20) // math.isqrt(rank ** lean) + 1 for rank in range(1, number_of + 1)]
    largest = limit if full else min(limit, max(-(-total // number_of), total * loads[0] // sum(loads)))
    least = 1 if total - largest >= number_of - 1 else 0
    given, surplus = [largest] + [least] * (number_of - 1), total - largest - least * (number_of - 1)
    while surplus > 0:
        candidates = [i for i in range(1, number_of) if given[i] < largest] or [i for i in range(1, number_of) if given[i] < limit]
        whole, remaining = sum([loads[i] for i in candidates]), surplus
        for i in candidates:
            more = min(limit - given[i], max(1, remaining * loads[i] // whole), surplus)
            given[i] = given[i] + more
            surplus = surplus - more
    return np.array(given)


def normal_values(key, extent, width, limit, pieces=(), held_as=jnp.bfloat16):
    gain = steps_of(key, extent, pieces, -0.22, 0.18) if pieces else 1.0
    result = jax.random.normal(key, extent, jnp.float32) * width * gain
    return jnp.minimum(jnp.maximum(result, -limit), limit).astype(held_as)


def setup_inputs(seed: int = 0) -> dict:
    key_of = jax.random.split(jax.random.key(seed), 12)
    hidden_in = normal_values(key_of[0], (TOKENS, D), 0.5, 4.0, ((0, 128),))
    queries = draw_queries(jax.random.fold_in(key_of[11], 71), 0)
    keys = draw_keys(jax.random.fold_in(key_of[11], 71), 0)
    values = normal_values(key_of[3], (TOKENS, KV * DH), 2.0, 8.0, ((0, 128),))
    out_weight = normal_values(key_of[4], (H * DH, D), (H * DH) ** -0.5, 0.09375, ((0, 8),))
    norm_gain = jnp.clip(1.0 + 0.1 * jax.random.normal(key_of[5], (D,), jnp.float32), 0.5, 1.5)
    routes_keys = jax.random.split(jax.random.fold_in(key_of[6], 1), TOKENS // TOK_DEV)
    routes_turns = jax.random.permutation(jax.random.fold_in(key_of[6], 3), TOKENS // TOK_DEV)
    routes = jax.vmap(lambda own, number: assign_block(jax.random.fold_in(key_of[6], 2), own, number, TOK_DEV, EXPERTS, TOP, CAP, 2))(routes_keys, routes_turns).reshape((TOKENS, TOP))
    gates = draw_gates(jax.random.fold_in(key_of[11], 71), 0)
    w_gate = normal_values(key_of[8], (EXPERTS, D, FF), D ** -0.5, 0.125, ((0, 128),))
    w_up = normal_values(key_of[9], (EXPERTS, D, FF), D ** -0.5, 0.125, ((0, 128),))
    w_down = normal_values(key_of[10], (EXPERTS, FF, D), FF ** -0.5, 0.21875, ((0, 128),))
    return dict(hidden_in=hidden_in, queries=queries, keys=keys, values=values, out_weight=out_weight, norm_gain=norm_gain, routes=routes, gates=gates, w_gate=w_gate, w_up=w_up, w_down=w_down)


def attend_sequence(queries, keys, values, index):
    first = index * SEQ
    qs = lax.dynamic_slice_in_dim(queries, first, SEQ, 0).astype(jnp.float32).reshape(SEQ, KV, H // KV, DH)
    ks = lax.dynamic_slice_in_dim(keys, first, SEQ, 0).astype(jnp.float32).reshape(SEQ, KV, DH)
    vs = lax.dynamic_slice_in_dim(values, first, SEQ, 0).astype(jnp.float32).reshape(SEQ, KV, DH)
    scores = jnp.einsum('qghd,kgd->ghqk', qs, ks) / math.sqrt(DH)
    rows = jnp.arange(SEQ, dtype=jnp.int32)[:, None]
    cols = jnp.arange(SEQ, dtype=jnp.int32)[None, :]
    scores = jnp.where(cols <= rows, scores, -jnp.inf)
    top_score = lax.optimization_barrier(jnp.max(scores, axis=-1, keepdims=True))
    expo = jnp.exp(scores - top_score)
    weights = (expo / lax.optimization_barrier(jnp.sum(expo, axis=-1, keepdims=True))).astype(jnp.bfloat16)
    out = jnp.einsum('ghqk,kgd->qghd', weights.astype(jnp.float32), vs)
    return out.astype(jnp.bfloat16).reshape(SEQ, H * DH)

def reference(hidden_in, queries, keys, values, out_weight, norm_gain, routes, gates, w_gate, w_up, w_down):
    heads_out = lax.map(lambda index: attend_sequence(queries, keys, values, index), jnp.arange(N_DP, dtype=jnp.int32))
    heads_out = heads_out.reshape(TOKENS, H * DH)
    residual_sum = hidden_in.astype(jnp.float32) + jnp.dot(heads_out, out_weight, preferred_element_type=jnp.float32)
    attended = residual_sum.astype(jnp.bfloat16)
    mean_square = lax.optimization_barrier(jnp.mean(residual_sum * residual_sum, axis=1, keepdims=True))
    normed = (residual_sum / jnp.sqrt(mean_square + 1e-06) * norm_gain).astype(jnp.bfloat16)
    flat_ids = routes.reshape(-1)
    flat_gates = gates.reshape(-1)
    rows_most = N_DP * N_CTX * CAP

    def per_expert(total, inputs):
        expert, gate_w, up_w, down_w = inputs
        chosen = flat_ids == expert
        count = jnp.sum(chosen.astype(jnp.int32))
        picked = jnp.nonzero(chosen, size=rows_most, fill_value=0)[0].astype(jnp.int32)
        live = jnp.arange(rows_most, dtype=jnp.int32) < count
        token_ids = picked // TOP
        rows_in = normed[token_ids]
        gate_act = jnp.dot(rows_in, gate_w, preferred_element_type=jnp.float32)
        up_act = jnp.dot(rows_in, up_w, preferred_element_type=jnp.float32)
        expert_hidden = (jax.nn.silu(gate_act) * up_act).astype(jnp.bfloat16)
        expert_rows = jnp.dot(expert_hidden, down_w, preferred_element_type=jnp.float32).astype(jnp.bfloat16)
        weight = jnp.where(live, flat_gates[picked], jnp.float32(0.0))
        total = total.at[token_ids].add(expert_rows.astype(jnp.float32) * weight[:, None])
        return (total, None)
    start_mix = jnp.zeros((TOKENS, D), jnp.float32)
    mixed, unused = lax.scan(per_expert, start_mix, (jnp.arange(EXPERTS, dtype=jnp.int32), w_gate, w_up, w_down))
    expert_mix = mixed.astype(jnp.bfloat16)
    onehot = (flat_ids[:, None] == jnp.arange(EXPERTS, dtype=jnp.int32)[None, :]).astype(jnp.float32)
    counts = lax.optimization_barrier(jnp.sum(onehot, axis=0))
    gate_sums = lax.optimization_barrier(jnp.sum(onehot * flat_gates[:, None], axis=0))
    balance_loss = EXPERTS * jnp.sum(counts / (TOKENS * TOP) * (gate_sums / TOKENS))
    expert_load = EXPERTS * counts / (TOKENS * TOP)
    return (attended, expert_mix, balance_loss, expert_load)
```

```python
import functools
import math

import jax
import jax.numpy as jnp
from jax import lax
from jax.experimental import pallas as pl
from jax.experimental.pallas import tpu as pltpu
from jax.sharding import PartitionSpec as P

H = 32
KV = 4
DH = 128
TOP = 8
D = 2048
FF = 768
TOK = 128
NE = 128
CTX = 8
GH = H // KV
HALF = 512
WHOLE = 8
CAP = 12
QUARTER = 256
WIDE = 3072
ALL = ("dp", "ctx")
Z_GROUPS = [[0, 2, 4, 6], [1, 3, 5, 7]]
BF = jnp.bfloat16
F32 = jnp.float32
VMEM_LIMIT = 56 * 1024 * 1024


def params(**more):
    return pltpu.CompilerParams(vmem_limit_bytes=VMEM_LIMIT, **more)


def dot(a, b):
    return jnp.dot(a, b, preferred_element_type=F32)


def route_kernel(routes_ref, gates_ref, pick1_ref, pick2_ref, mix1_ref, mix2_ref, stat_ref):
    experts = lax.broadcasted_iota(jnp.int32, (NE, TOK), 0)
    named = jnp.zeros((NE, TOK), F32)
    weight = jnp.zeros((NE, TOK), F32)
    for k in range(TOP):
        hit = routes_ref[k : k + 1, :] == experts
        named = jnp.where(hit, 1.0, named)
        weight = jnp.where(hit, gates_ref[k : k + 1, :], weight)
    earlier = lax.broadcasted_iota(jnp.int32, (TOK, TOK), 0) < lax.broadcasted_iota(
        jnp.int32, (TOK, TOK), 1
    )
    rank = dot(named.astype(BF), earlier.astype(F32).astype(BF))
    rank = jnp.where(named > 0, rank, -1.0)
    rank = jnp.broadcast_to(rank[:, None, :], (NE, 8, TOK)).reshape(NE * 8, TOK)
    weights = jnp.broadcast_to(weight[:, None, :], (NE, 8, TOK)).reshape(NE * 8, TOK)
    row = lax.broadcasted_iota(jnp.int32, (NE * 8, TOK), 0) & 7
    pick1 = rank == row.astype(F32)
    pick1_ref[...] = jnp.where(pick1, 1.0, 0.0).astype(BF)
    base = rank == (WHOLE + (row & 3)).astype(F32)
    left = base & (row < 4)
    right = base & (row >= 4)
    pick2_ref[:, :TOK] = jnp.where(left, 1.0, 0.0).astype(BF)
    pick2_ref[:, TOK:] = jnp.where(right, 1.0, 0.0).astype(BF)

    def put(ref, first, chosen):
        mix = jnp.transpose(jnp.where(chosen, weights, 0.0))
        high = mix.astype(BF)
        ref[first : first + TOK, :] = high
        ref[first + TOK : first + 2 * TOK, :] = (mix - high.astype(F32)).astype(BF)

    put(mix1_ref, 0, pick1)
    put(mix2_ref, 0, left)
    put(mix2_ref, 2 * TOK, right)
    stat_ref[...] = jnp.zeros((8, NE), F32)
    stat_ref[0:1, :] = jnp.sum(jnp.transpose(named), axis=0, keepdims=True)
    total = jnp.sum(jnp.transpose(weight), axis=0, keepdims=True)
    high = total.astype(BF).astype(F32)
    stat_ref[1:2, :] = high
    stat_ref[2:3, :] = total - high


def route_plan(routes, gates):
    return pl.pallas_call(
        route_kernel,
        out_shape=(
            jax.ShapeDtypeStruct((NE * 8, TOK), BF),
            jax.ShapeDtypeStruct((NE * 8, 2 * TOK), BF),
            jax.ShapeDtypeStruct((2 * TOK, NE * 8), BF),
            jax.ShapeDtypeStruct((4 * TOK, NE * 8), BF),
            jax.ShapeDtypeStruct((8, NE), F32),
        ),
        compiler_params=params(),
        name="route_plan",
    )(routes.T, gates.T)


def attend_kernel(half_ref, q_ref, kv_ref, out_ref):
    half = half_ref[0]
    keys = kv_ref[:, :DH]
    values = jnp.concatenate([kv_ref[:, DH:], jnp.ones((CTX * TOK, DH), BF)], axis=1)
    scale = math.log2(math.e) / math.sqrt(DH)
    rows = half * TOK + lax.broadcasted_iota(jnp.int32, (TOK, 2 * TOK), 0)
    seen = lax.broadcasted_iota(jnp.int32, (TOK, 2 * TOK), 1) <= rows
    for block in range(4):
        whole = block * 2 * TOK
        for head in range(GH):
            part, inner = divmod(head, GH // 2)
            first = (part ^ half) * HALF + inner * DH if part == 0 else (1 - half) * HALF + inner * DH
            q = q_ref[block, :, pl.ds(pl.multiple_of(first, DH), DH)]
            tail = lax.dot_general(
                q,
                keys[whole : whole + 2 * TOK],
                (((1,), (1,)), ((), ())),
                preferred_element_type=F32,
            )
            tail = jnp.where(seen, tail, -jnp.inf)
            top = jnp.max(tail, axis=1, keepdims=True)
            if block:
                body = lax.dot_general(
                    q, keys[:whole], (((1,), (1,)), ((), ())), preferred_element_type=F32
                )
                top = jnp.maximum(top, jnp.max(body, axis=1, keepdims=True))
            expo = jnp.exp2((tail - top) * scale).astype(BF)
            result = dot(expo, values[whole : whole + 2 * TOK])
            if block:
                expo = jnp.exp2((body - top) * scale).astype(BF)
                result = result + dot(expo, values[:whole])
            out_ref[block, :, head * DH : (head + 1) * DH] = (
                result[:, :DH] / result[:, DH:]
            ).astype(BF)


def attend(half, q, kv):
    return pl.pallas_call(
        attend_kernel,
        out_shape=jax.ShapeDtypeStruct(q.shape, BF),
        in_specs=[
            pl.BlockSpec(memory_space=pltpu.SMEM),
            pl.BlockSpec(memory_space=pltpu.VMEM),
            pl.BlockSpec(memory_space=pltpu.VMEM),
        ],
        out_specs=pl.BlockSpec(memory_space=pltpu.VMEM),
        compiler_params=params(),
        cost_estimate=pl.CostEstimate(
            flops=2 * 2 * 512 * 8 * 640 * 128, bytes_accessed=3 << 20, transcendentals=512 * 8 * 640
        ),
        name="attend",
    )(half, q, kv)


def project_kernel(core_ref, heads_ref, mine_ref, near_ref, far_ref, out_ref):
    core = core_ref[0]
    near = HALF + core * QUARTER
    far = HALF + (1 - core) * QUARTER
    total = dot(heads_ref[:, :HALF], mine_ref[...])
    total = total + dot(heads_ref[:, pl.ds(pl.multiple_of(near, QUARTER), QUARTER)], near_ref[...])
    total = total + dot(heads_ref[:, pl.ds(pl.multiple_of(far, QUARTER), QUARTER)], far_ref[...])
    out_ref[...] = total.astype(BF)


def project(core, heads, mine, near, far):
    rows, cols = heads.shape[0], 512
    return pl.pallas_call(
        project_kernel,
        grid=(D // cols,),
        out_shape=jax.ShapeDtypeStruct((rows, D), BF),
        in_specs=[
            pl.BlockSpec(memory_space=pltpu.SMEM),
            pl.BlockSpec((rows, 2 * HALF), lambda j: (0, 0)),
            pl.BlockSpec((HALF, cols), lambda j: (0, j)),
            pl.BlockSpec((QUARTER, cols), lambda j: (0, j)),
            pl.BlockSpec((QUARTER, cols), lambda j: (0, j)),
        ],
        out_specs=pl.BlockSpec((rows, cols), lambda j: (0, j)),
        compiler_params=params(),
        cost_estimate=pl.CostEstimate(
            flops=2 * rows * 2 * HALF * D, bytes_accessed=8 << 20, transcendentals=0
        ),
        name="project",
    )(core, heads, mine, near, far)


def residual_kernel(
    parts_ref, hidden_ref, gain_ref, pick1_ref, pick2_ref, att_ref, x_ref, norm_ref, stack_ref
):
    @pl.when(pl.program_id(0) == 0)
    def _():
        total = hidden_ref[...].astype(F32)
        for part in range(4):
            total = total + parts_ref[part].astype(F32)
        att_ref[...] = total.astype(BF)
        square = jnp.mean(total * total, axis=1, keepdims=True)
        normed = (total / jnp.sqrt(square + 1e-06) * gain_ref[...]).astype(BF)
        norm_ref[...] = normed
        stack_ref[:TOK, :] = normed[:, : D // 2]
        stack_ref[TOK:, :] = normed[:, D // 2 :]

    x_ref[:, :D] = dot(pick1_ref[...], norm_ref[...]).astype(BF)
    x_ref[:, D:] = dot(pick2_ref[...], stack_ref[...]).astype(BF)


def residual(parts, hidden, gain, pick1, pick2):
    steps = 4
    rows = NE * 8 // steps
    return pl.pallas_call(
        residual_kernel,
        grid=(steps,),
        out_shape=(
            jax.ShapeDtypeStruct((TOK, D), BF),
            jax.ShapeDtypeStruct((NE * 8, WIDE), BF),
        ),
        in_specs=[
            pl.BlockSpec((4, TOK, D), lambda i: (0, 0, 0)),
            pl.BlockSpec((TOK, D), lambda i: (0, 0)),
            pl.BlockSpec((1, D), lambda i: (0, 0)),
            pl.BlockSpec((rows, TOK), lambda i: (i, 0)),
            pl.BlockSpec((rows, 2 * TOK), lambda i: (i, 0)),
        ],
        out_specs=(
            pl.BlockSpec((TOK, D), lambda i: (0, 0)),
            pl.BlockSpec((rows, WIDE), lambda i: (i, 0)),
        ),
        scratch_shapes=[pltpu.VMEM((TOK, D), BF), pltpu.VMEM((2 * TOK, D // 2), BF)],
        compiler_params=params(),
        cost_estimate=pl.CostEstimate(flops=1 << 30, bytes_accessed=10 << 20, transcendentals=128),
        name="residual_norm_pick",
    )(parts, hidden, gain.reshape(1, D), pick1, pick2)


def expert_kernel(x_ref, gate_ref, up_ref, down_ref, stat_ref, y_ref):
    rows = x_ref.shape[0]
    count = rows // 2
    half = D // 2
    to = lax.broadcasted_iota(jnp.int32, (rows, rows), 0)
    at = lax.broadcasted_iota(jnp.int32, (rows, rows), 1)

    def source(i):
        side = (i >= count).astype(jnp.int32)
        own = i - side * count
        return (own >> 2) * 8 + side * 4 + (own & 3)

    sort = jnp.where(source(to) == at, 1.0, 0.0).astype(BF)
    back = jnp.where(source(at) == to, 1.0, 0.0).astype(BF)
    rest = dot(sort, x_ref[:, D:]).astype(BF)
    rest = jnp.concatenate([rest[:count], rest[count:]], axis=1)
    x = jnp.concatenate([x_ref[:, :D], rest], axis=0)
    gate = dot(x, gate_ref[0])
    hidden = (gate / (1.0 + jnp.exp(-gate)) * dot(x, up_ref[0])).astype(BF)
    y = dot(hidden, down_ref[0]).astype(BF)
    y_ref[:, :D] = y[:rows]
    rest = jnp.concatenate([y[rows:, :half], y[rows:, half:]], axis=0)
    y_ref[:, D:WIDE] = dot(back, rest).astype(BF)
    stat = jnp.broadcast_to(stat_ref[...][None], (rows // 8, 8, NE)).reshape(rows, NE)
    y_ref[:, WIDE:] = stat.astype(BF)


def expert_apply(x, w_gate, w_up, w_down, stat):
    rows = 256
    return pl.pallas_call(
        expert_kernel,
        grid=(NE * 8 // rows,),
        out_shape=jax.ShapeDtypeStruct((NE * 8, WIDE + NE), BF),
        in_specs=[
            pl.BlockSpec((rows, WIDE), lambda i: (i, 0)),
            pl.BlockSpec((1, D, FF), lambda i: (0, 0, 0)),
            pl.BlockSpec((1, D, FF), lambda i: (0, 0, 0)),
            pl.BlockSpec((1, FF, D), lambda i: (0, 0, 0)),
            pl.BlockSpec((8, NE), lambda i: (0, 0)),
        ],
        out_specs=pl.BlockSpec((rows, WIDE + NE), lambda i: (i, 0)),
        compiler_params=params(),
        cost_estimate=pl.CostEstimate(
            flops=6 * NE * CAP * D * FF, bytes_accessed=22 << 20, transcendentals=NE * CAP * FF
        ),
        name="experts",
    )(x, w_gate, w_up, w_down, stat)


def mix_kernel(mix1_ref, mix2_ref, y_ref, rest_ref, stat_ref, out_ref, load_ref, loss_ref):
    both = dot(mix1_ref[...], y_ref[...]) + dot(mix2_ref[...], rest_ref[...])
    out_ref[...] = (both[:TOK] + both[TOK:]).astype(BF)

    @pl.when(pl.program_id(0) == 0)
    def _():
        stat = jnp.sum(stat_ref[...].astype(F32).reshape(NE, 8, NE), axis=0)
        counts = stat[0:1]
        gates = stat[1:2] + stat[2:3]
        tokens = TOK * NE
        load = counts / (tokens * TOP)
        load_ref[...] = NE * load
        loss = NE * jnp.sum(load * (gates / tokens), axis=1, keepdims=True)
        loss_ref[...] = jnp.broadcast_to(loss, (1, NE))


def mix(mix1, mix2, y):
    cols = 512
    return pl.pallas_call(
        mix_kernel,
        grid=(D // cols,),
        out_shape=(
            jax.ShapeDtypeStruct((TOK, D), BF),
            jax.ShapeDtypeStruct((1, NE), F32),
            jax.ShapeDtypeStruct((1, NE), F32),
        ),
        in_specs=[
            pl.BlockSpec((2 * TOK, NE * 8), lambda j: (0, 0)),
            pl.BlockSpec((2 * TOK, NE * 8), lambda j: (j // 2, 0)),
            pl.BlockSpec((NE * 8, cols), lambda j: (0, j)),
            pl.BlockSpec((NE * 8, cols), lambda j: (0, D // cols + j % 2)),
            pl.BlockSpec((NE * 8, NE), lambda j: (0, WIDE // NE)),
        ],
        out_specs=(
            pl.BlockSpec((TOK, cols), lambda j: (0, j)),
            pl.BlockSpec((1, NE), lambda j: (0, 0)),
            pl.BlockSpec((1, NE), lambda j: (0, 0)),
        ),
        compiler_params=params(),
        cost_estimate=pl.CostEstimate(flops=2 << 30, bytes_accessed=8 << 20, transcendentals=0),
        name="mix",
    )(mix1, mix2, y, y, y)


def swap(x, axis, count, step):
    return lax.ppermute(x, axis, [(i, i ^ step) for i in range(count)])


def exchange(x, axes, groups=None):
    return lax.all_to_all(
        x, axes, split_axis=0, concat_axis=0, tiled=True, axis_index_groups=groups
    )


def on_device(
    hidden_in, queries, keys, values, out_weight, norm_gain, routes, gates, w_gate, w_up, w_down
):
    half = (lax.axis_index("ctx") % 2).astype(jnp.int32).reshape(1)
    kv = jnp.concatenate([keys.reshape(TOK, KV, DH), values.reshape(TOK, KV, DH)], axis=2)
    kv = jnp.transpose(kv, (1, 0, 2))
    kv = jnp.broadcast_to(kv[:, None], (KV, 2, TOK, 2 * DH)).reshape(CTX, TOK, 2 * DH)
    kv = exchange(kv, "ctx")
    q = jnp.transpose(queries.reshape(TOK, KV, GH * DH), (1, 0, 2))
    q = exchange(q, "ctx", Z_GROUPS)
    core = (lax.axis_index("dp") % 2).astype(jnp.int32).reshape(1)
    near = lax.dynamic_slice_in_dim(out_weight, core[0] * QUARTER, QUARTER, 0)
    near = swap(near, "ctx", CTX, 1)
    far = swap(near, "dp", 16, 1)
    pick1, pick2, mix1, mix2, stat = route_plan(routes, gates)
    heads = attend(half, q, kv.reshape(CTX * TOK, 2 * DH))
    partial = project(core, heads.reshape(4 * TOK, GH * DH), out_weight, near, far)
    parts = exchange(partial.reshape(4, TOK, D), "ctx", Z_GROUPS)
    attended, x = residual(parts, hidden_in, norm_gain, pick1, pick2)
    x = exchange(x.reshape(NE, 8, WIDE), ALL)
    y = expert_apply(x.reshape(NE * 8, WIDE), w_gate, w_up, w_down, stat)
    y = exchange(y.reshape(NE, 8, WIDE + NE), ALL)
    expert_mix, load, loss = mix(mix1, mix2, y.reshape(NE * 8, WIDE + NE))
    return attended, expert_mix, loss[0, 0], load[0]


def solution(mesh):
    rows = P(ALL, None)
    return jax.shard_map(
        on_device,
        mesh=mesh,
        in_specs=(
            rows,
            rows,
            rows,
            rows,
            P("ctx", None),
            P(),
            rows,
            rows,
            P(ALL, None, None),
            P(ALL, None, None),
            P(ALL, None, None),
        ),
        out_specs=(rows, rows, P(), P()),
        check_vma=False,
    )
```

```python
import functools
import math

import jax
import jax.numpy as jnp
from jax import lax
from jax.experimental import pallas as pl
from jax.experimental.pallas import tpu as pltpu
from jax.sharding import PartitionSpec as P

H = 32
KV = 4
DH = 128
TOP = 8
D = 2048
FF = 768
TOK = 128
NE = 128
CTX = 8
GH = H // KV
SENT = GH * DH + 4 * DH
HALF = 512
WHOLE = 8
CAP = 12
QUARTER = 256
WIDE = 3072
ALL = ("dp", "ctx")
Z_GROUPS = [[0, 2, 4, 6], [1, 3, 5, 7]]
BF = jnp.bfloat16
F32 = jnp.float32
def params(megabytes):
    return pltpu.CompilerParams(vmem_limit_bytes=megabytes << 20)


def near_core(x):
    return pltpu.with_memory_space_constraint(x, pltpu.VMEM)


def far_memory(x):
    return pltpu.with_memory_space_constraint(x, pltpu.HBM)


ANY = pl.BlockSpec(memory_space=pl.ANY)
VM = pl.BlockSpec(memory_space=pltpu.VMEM)
SM = pl.BlockSpec(memory_space=pltpu.SMEM)


def dot(a, b):
    return jnp.dot(a, b, preferred_element_type=F32)


def route_kernel(routes_ref, gates_ref, pick1_ref, pick2_ref, mix1_ref, mix2_ref, stat_ref):
    experts = lax.broadcasted_iota(jnp.int32, (NE, TOK), 0)
    named = jnp.zeros((NE, TOK), F32)
    weight = jnp.zeros((NE, TOK), F32)
    for k in range(TOP):
        hit = routes_ref[k : k + 1, :] == experts
        named = jnp.where(hit, 1.0, named)
        weight = jnp.where(hit, gates_ref[k : k + 1, :], weight)
    earlier = lax.broadcasted_iota(jnp.int32, (TOK, TOK), 0) < lax.broadcasted_iota(
        jnp.int32, (TOK, TOK), 1
    )
    rank = dot(named.astype(BF), earlier.astype(F32).astype(BF))
    rank = jnp.where(named > 0, rank, -1.0)
    rank = jnp.broadcast_to(rank[:, None, :], (NE, 8, TOK)).reshape(NE * 8, TOK)
    weights = jnp.broadcast_to(weight[:, None, :], (NE, 8, TOK)).reshape(NE * 8, TOK)
    row = lax.broadcasted_iota(jnp.int32, (NE * 8, TOK), 0) & 7
    pick1 = rank == row.astype(F32)
    pick1_ref[...] = jnp.where(pick1, 1.0, 0.0).astype(BF)
    base = rank == (WHOLE + (row & 3)).astype(F32)
    left = base & (row < 4)
    right = base & (row >= 4)
    pick2_ref[:, :TOK] = jnp.where(left, 1.0, 0.0).astype(BF)
    pick2_ref[:, TOK:] = jnp.where(right, 1.0, 0.0).astype(BF)

    def put(ref, first, chosen):
        mix = jnp.transpose(jnp.where(chosen, weights, 0.0))
        high = mix.astype(BF)
        ref[first : first + TOK, :] = high
        ref[first + TOK : first + 2 * TOK, :] = (mix - high.astype(F32)).astype(BF)

    put(mix1_ref, 0, pick1)
    put(mix2_ref, 0, left)
    put(mix2_ref, 2 * TOK, right)
    stat_ref[...] = jnp.zeros((8, NE), F32)
    stat_ref[0:1, :] = jnp.sum(jnp.transpose(named), axis=0, keepdims=True)
    total = jnp.sum(jnp.transpose(weight), axis=0, keepdims=True)
    high = total.astype(BF).astype(F32)
    stat_ref[1:2, :] = high
    stat_ref[2:3, :] = total - high


def route_plan(routes, gates):
    return pl.pallas_call(
        route_kernel,
        out_shape=(
            pltpu.HBM((NE * 8, TOK), BF),
            pltpu.HBM((NE * 8, 2 * TOK), BF),
            pltpu.HBM((2 * TOK, NE * 8), BF),
            pltpu.HBM((4 * TOK, NE * 8), BF),
            pltpu.HBM((8, NE), F32),
        ),
        in_specs=[VM] * 2,
        out_specs=(VM,) * 5,
        compiler_params=params(8),
        name="route_plan",
    )(routes.T, gates.T)


def send_kernel(q_ref, keys_ref, values_ref, partner_keys_ref, partner_values_ref, out_ref):
    parts = (keys_ref, values_ref, partner_keys_ref, partner_values_ref)
    wide = GH * DH
    for group in range(KV):
        out_ref[group, :, :wide] = q_ref[:, group * wide : (group + 1) * wide]
        for i, ref in enumerate(parts):
            first = wide + i * DH
            out_ref[group, :, first : first + DH] = ref[:, group * DH : (group + 1) * DH]


def send_rows(*arrays):
    return pl.pallas_call(
        send_kernel,
        out_shape=jax.ShapeDtypeStruct((KV, TOK, SENT), BF),
        in_specs=[VM] * 5,
        out_specs=VM,
        compiler_params=params(4),
        name="send_rows",
    )(*(near_core(x) for x in arrays))


def send_weight_kernel(core_ref, weight_ref, first_ref, second_ref, out_ref, sem):
    del first_ref, second_ref
    rows = pl.ds(pl.multiple_of(core_ref[0] * QUARTER, QUARTER), QUARTER)
    copy = pltpu.make_async_copy(weight_ref.at[rows], out_ref, sem)
    copy.start()
    copy.wait()


def send_weight(core, weight, first, second):
    return pl.pallas_call(
        send_weight_kernel,
        out_shape=jax.ShapeDtypeStruct((QUARTER, D), BF),
        in_specs=[SM, ANY, ANY, ANY],
        out_specs=ANY,
        scratch_shapes=[pltpu.SemaphoreType.DMA],
        compiler_params=params(4),
        name="send_weight",
    )(core, weight, first, second)


def attend_kernel(half_ref, sent_ref, out_ref):
    half = half_ref[0]
    one = jnp.ones((4 * TOK, DH), BF)

    def piece(i):
        first = GH * DH + i * DH
        return jnp.concatenate([sent_ref[z, :, first : first + DH] for z in range(4)], axis=0)

    keys = [piece(0), piece(2)]
    values = [jnp.concatenate([piece(i), one], axis=1) for i in (1, 3)]
    scale = math.log2(math.e) / math.sqrt(DH)
    below = lax.broadcasted_iota(jnp.int32, (TOK, TOK), 1) <= lax.broadcasted_iota(
        jnp.int32, (TOK, TOK), 0
    )
    for block in range(4):
        upto = (block + 1) * TOK
        for head in range(GH):
            part, inner = divmod(head, GH // 2)
            first = (half if part == 0 else 1 - half) * HALF + inner * DH
            q = sent_ref[block, :, pl.ds(pl.multiple_of(first, DH), DH)]
            scores = []
            for side in range(2):
                score = lax.dot_general(
                    q, keys[side][:upto], (((1,), (1,)), ((), ())), preferred_element_type=F32
                )
                seen = below if side == 0 else jnp.full((TOK, TOK), half, jnp.int32) == 1
                last = jnp.where(seen, score[:, upto - TOK :], -jnp.inf)
                if block:
                    last = jnp.concatenate([score[:, : upto - TOK], last], axis=1)
                scores.append(last)
            top = jnp.maximum(
                jnp.max(scores[0], axis=1, keepdims=True), jnp.max(scores[1], axis=1, keepdims=True)
            )
            result = 0.0
            for side in range(2):
                expo = jnp.exp2((scores[side] - top) * scale).astype(BF)
                result = result + dot(expo, values[side][:upto])
            out_ref[block, :, head * DH : (head + 1) * DH] = (
                result[:, :DH] / result[:, DH:]
            ).astype(BF)


def attend(half, sent):
    return pl.pallas_call(
        attend_kernel,
        out_shape=pltpu.VMEM((4, TOK, GH * DH), BF),
        in_specs=[SM, VM],
        out_specs=VM,
        compiler_params=params(16),
        cost_estimate=pl.CostEstimate(
            flops=2 * 2 * 512 * 8 * 640 * 128, bytes_accessed=3 << 20, transcendentals=512 * 8 * 640
        ),
        name="attend",
    )(half, near_core(sent))


def project_mine_kernel(heads_ref, mine_ref, out_ref):
    heads = heads_ref[:, :, :HALF].reshape(4 * TOK, HALF)
    cols = 512
    for j in range(0, D, cols):
        total = dot(heads, mine_ref[:, j : j + cols])
        out_ref[:, :, j : j + cols] = total.reshape(4, TOK, cols)


def project_mine(heads, mine):
    return pl.pallas_call(
        project_mine_kernel,
        out_shape=pltpu.VMEM((4, TOK, D), F32),
        in_specs=[VM] * 2,
        out_specs=VM,
        compiler_params=params(8),
        cost_estimate=pl.CostEstimate(
            flops=2 * 4 * TOK * HALF * D, bytes_accessed=8 << 20, transcendentals=0
        ),
        name="project_mine",
    )(near_core(heads), near_core(mine))


def project_kernel(steps, place_ref, heads_ref, mine_ref, near_ref, far_ref, *out_refs):
    core = place_ref[0]
    blocks = [(place_ref[1] + step) % 4 for step in steps]
    near = pl.multiple_of(HALF + core * QUARTER, QUARTER)
    far = pl.multiple_of(HALF + (1 - core) * QUARTER, QUARTER)

    def heads(first):
        rows = [heads_ref[block, :, pl.ds(first, QUARTER)] for block in blocks]
        return rows[0] if len(rows) == 1 else jnp.concatenate(rows, axis=0)

    second, third = heads(near), heads(far)
    cols = 512
    for j in range(0, D, cols):
        total = dot(second, near_ref[:, j : j + cols]) + dot(third, far_ref[:, j : j + cols])
        for i, block in enumerate(blocks):
            out = total[i * TOK : (i + 1) * TOK] + mine_ref[block, :, j : j + cols]
            out_refs[i][:, j : j + cols] = out.astype(out_refs[i].dtype)


def project(steps, kind, place, heads, mine, near, far):
    return pl.pallas_call(
        functools.partial(project_kernel, steps),
        out_shape=[pltpu.VMEM((TOK, D), kind)] * len(steps),
        in_specs=[SM] + [VM] * 4,
        out_specs=[VM] * len(steps),
        compiler_params=params(8),
        cost_estimate=pl.CostEstimate(
            flops=2 * len(steps) * TOK * HALF * D, bytes_accessed=8 << 20, transcendentals=0
        ),
        name="project",
    )(place, near_core(heads), near_core(mine), near_core(near), near_core(far))


def residual_kernel(
    own_ref, one_ref, two_ref, three_ref, hidden_any, gain_ref, pick1_any, pick2_any,
    att_ref, x_ref, hidden_ref, pick1_ref, pick2_ref, sems
):
    pairs = ((hidden_any, hidden_ref), (pick1_any, pick1_ref), (pick2_any, pick2_ref))
    copies = [pltpu.make_async_copy(a, b, sems.at[i]) for i, (a, b) in enumerate(pairs)]
    for copy in copies:
        copy.start()
    total = own_ref[...] + one_ref[...].astype(F32)
    total = total + (two_ref[...].astype(F32) + three_ref[...].astype(F32))
    copies[0].wait()
    total = total + hidden_ref[...].astype(F32)
    att_ref[...] = total.astype(BF)
    square = jnp.mean(total * total, axis=1, keepdims=True)
    normed = (total / jnp.sqrt(square + 1e-06) * gain_ref[...]).astype(BF)
    stack = jnp.concatenate([normed[:, : D // 2], normed[:, D // 2 :]], axis=0)
    copies[1].wait()
    copies[2].wait()
    rows = 256
    for first in range(0, NE * 8, rows):
        x_ref[first : first + rows, :D] = dot(pick1_ref[first : first + rows], normed).astype(BF)
        x_ref[first : first + rows, D:] = dot(pick2_ref[first : first + rows], stack).astype(BF)


def residual(sums, hidden, gain, pick1, pick2):
    return pl.pallas_call(
        residual_kernel,
        out_shape=(jax.ShapeDtypeStruct((TOK, D), BF), pltpu.VMEM((NE * 8, WIDE), BF)),
        in_specs=[VM] * 4 + [ANY, VM, ANY, ANY],
        out_specs=(VM, VM),
        scratch_shapes=[
            pltpu.VMEM(hidden.shape, BF),
            pltpu.VMEM(pick1.shape, BF),
            pltpu.VMEM(pick2.shape, BF),
            pltpu.SemaphoreType.DMA((3,)),
        ],
        compiler_params=params(12),
        cost_estimate=pl.CostEstimate(flops=1 << 30, bytes_accessed=10 << 20, transcendentals=128),
        name="residual_norm_pick",
    )(
        *(near_core(x) for x in sums),
        far_memory(hidden),
        gain.reshape(1, D),
        far_memory(pick1),
        far_memory(pick2),
    )


def expert_kernel(x_ref, gate_ref, up_ref, down_ref, stat_ref, y_ref):
    rows = 256
    count = rows // 2
    half = D // 2
    to = lax.broadcasted_iota(jnp.int32, (rows, rows), 0)
    at = lax.broadcasted_iota(jnp.int32, (rows, rows), 1)

    def source(i):
        side = (i >= count).astype(jnp.int32)
        own = i - side * count
        return (own >> 2) * 8 + side * 4 + (own & 3)

    sort = jnp.where(source(to) == at, 1.0, 0.0).astype(BF)
    back = jnp.where(source(at) == to, 1.0, 0.0).astype(BF)
    stat = jnp.broadcast_to(stat_ref[...][None], (rows // 8, 8, NE)).reshape(rows, NE).astype(BF)

    def step(i, carry):
        span = pl.ds(pl.multiple_of(i * rows, rows), rows)
        rest = dot(sort, x_ref[span, D:]).astype(BF)
        rest = jnp.concatenate([rest[:count], rest[count:]], axis=1)
        x = jnp.concatenate([x_ref[span, :D], rest], axis=0)
        gate = dot(x, gate_ref[0])
        hidden = (gate / (1.0 + jnp.exp(-gate)) * dot(x, up_ref[0])).astype(BF)
        y = dot(hidden, down_ref[0]).astype(BF)
        y_ref[span, :D] = y[:rows]
        rest = jnp.concatenate([y[rows:, :half], y[rows:, half:]], axis=0)
        y_ref[span, D:WIDE] = dot(back, rest).astype(BF)
        y_ref[span, WIDE:] = stat
        return carry

    lax.fori_loop(0, NE * 8 // rows, step, 0)


def expert_apply(x, w_gate, w_up, w_down, stat):
    return pl.pallas_call(
        expert_kernel,
        out_shape=pltpu.VMEM((NE * 8, WIDE + NE), BF),
        in_specs=[VM] * 5,
        out_specs=VM,
        compiler_params=params(16),
        cost_estimate=pl.CostEstimate(
            flops=6 * NE * CAP * D * FF, bytes_accessed=22 << 20, transcendentals=NE * CAP * FF
        ),
        name="experts",
    )(near_core(x), near_core(w_gate), near_core(w_up), near_core(w_down), near_core(stat))


def mix_kernel(mix1_ref, mix2_ref, y_ref, out_ref, load_ref, loss_ref):
    cols = 512
    for j in range(D // cols):
        at = j * cols
        side = (j // 2) * 2 * TOK
        rest = D + (j % 2) * cols
        both = dot(mix1_ref[...], y_ref[:, at : at + cols])
        both = both + dot(mix2_ref[side : side + 2 * TOK], y_ref[:, rest : rest + cols])
        out_ref[:, at : at + cols] = (both[:TOK] + both[TOK:]).astype(BF)
    stat = jnp.sum(y_ref[:, WIDE:].astype(F32).reshape(NE, 8, NE), axis=0)
    counts = stat[0:1]
    gates = stat[1:2] + stat[2:3]
    tokens = TOK * NE
    load = counts / (tokens * TOP)
    load_ref[...] = NE * load
    loss = NE * jnp.sum(load * (gates / tokens), axis=1, keepdims=True)
    loss_ref[...] = jnp.broadcast_to(loss, (1, NE))


def mix(mix1, mix2, y):
    return pl.pallas_call(
        mix_kernel,
        out_shape=(
            jax.ShapeDtypeStruct((TOK, D), BF),
            jax.ShapeDtypeStruct((1, NE), F32),
            jax.ShapeDtypeStruct((1, NE), F32),
        ),
        in_specs=[VM] * 3,
        out_specs=(VM,) * 3,
        compiler_params=params(12),
        cost_estimate=pl.CostEstimate(flops=2 << 30, bytes_accessed=8 << 20, transcendentals=0),
        name="mix",
    )(near_core(mix1), near_core(mix2), near_core(y))


def swap(x, axis, count, step):
    return lax.ppermute(x, axis, [(i, i ^ step) for i in range(count)])


def turn(x, step):
    return lax.ppermute(x, "ctx", [(i, (i + 2 * step) % CTX) for i in range(CTX)])


def exchange(x, axes, groups=None):
    return lax.all_to_all(
        x, axes, split_axis=0, concat_axis=0, tiled=True, axis_index_groups=groups
    )


def on_device(
    hidden_in, queries, keys, values, out_weight, norm_gain, routes, gates, w_gate, w_up, w_down
):
    place = lax.axis_index("ctx").astype(jnp.int32)
    half = (place % 2).reshape(1)
    core = (lax.axis_index("dp") % 2).astype(jnp.int32).reshape(1)
    place = jnp.concatenate([core, (place // 2).reshape(1)])
    partner_keys = swap(keys, "ctx", CTX, 1)
    partner_values = swap(values, "ctx", CTX, 1)
    sent = send_rows(queries, keys, values, partner_keys, partner_values)
    sent = exchange(sent, "ctx", Z_GROUPS)
    near = swap(send_weight(core, out_weight, partner_keys, partner_values), "ctx", CTX, 1)
    far = swap(near, "dp", 16, 1)
    pick1, pick2, mix1, mix2, stat = route_plan(routes, gates)
    heads = attend(half, sent)
    mine = project_mine(heads, out_weight)
    (two,) = project((2,), BF, place, heads, mine, near, far)
    two = turn(two, 2)
    one, three = project((1, 3), BF, place, heads, mine, near, far)
    one, three = turn(one, 1), turn(three, 3)
    (own,) = project((0,), F32, place, heads, mine, near, far)
    attended, x = residual((own, one, two, three), hidden_in, norm_gain, pick1, pick2)
    x = exchange(x.reshape(NE, 8, WIDE), ALL)
    y = expert_apply(x.reshape(NE * 8, WIDE), w_gate, w_up, w_down, stat)
    y = exchange(y.reshape(NE, 8, WIDE + NE), ALL)
    expert_mix, load, loss = mix(mix1, mix2, y.reshape(NE * 8, WIDE + NE))
    return attended, expert_mix, loss[0, 0], load[0]


def solution(mesh):
    rows = P(ALL, None)
    return jax.shard_map(
        on_device,
        mesh=mesh,
        in_specs=(
            rows,
            rows,
            rows,
            rows,
            P("ctx", None),
            P(),
            rows,
            rows,
            P(ALL, None, None),
            P(ALL, None, None),
            P(ALL, None, None),
        ),
        out_specs=(rows, rows, P(), P()),
        check_vma=False,
    )
```

```python
import functools
import math

import jax
import jax.numpy as jnp
from jax import lax
from jax.experimental import pallas as pl
from jax.experimental.pallas import tpu as pltpu
from jax.sharding import PartitionSpec as P

H = 32
KV = 4
DH = 128
TOP = 8
D = 2048
FF = 768
TOK = 128
NE = 128
CTX = 8
GH = H // KV
SENT = GH * DH + 2 * DH
HALF = 512
WHOLE = 8
CAP = 12
QUARTER = 256
WIDE = 3072
ALL = ("dp", "ctx")
BF = jnp.bfloat16
F32 = jnp.float32
def params(megabytes):
    return pltpu.CompilerParams(vmem_limit_bytes=megabytes << 20)


def near_core(x):
    return pltpu.with_memory_space_constraint(x, pltpu.VMEM)


def far_memory(x):
    return pltpu.with_memory_space_constraint(x, pltpu.HBM)


ANY = pl.BlockSpec(memory_space=pl.ANY)
VM = pl.BlockSpec(memory_space=pltpu.VMEM)
SM = pl.BlockSpec(memory_space=pltpu.SMEM)


def dot(a, b):
    return jnp.dot(a, b, preferred_element_type=F32)


def route_kernel(routes_ref, gates_ref, pick1_ref, pick2_ref, mix1_ref, mix2_ref, stat_ref):
    experts = lax.broadcasted_iota(jnp.int32, (NE, TOK), 0)
    named = jnp.zeros((NE, TOK), F32)
    weight = jnp.zeros((NE, TOK), F32)
    for k in range(TOP):
        hit = routes_ref[k : k + 1, :] == experts
        named = jnp.where(hit, 1.0, named)
        weight = jnp.where(hit, gates_ref[k : k + 1, :], weight)
    earlier = lax.broadcasted_iota(jnp.int32, (TOK, TOK), 0) < lax.broadcasted_iota(
        jnp.int32, (TOK, TOK), 1
    )
    rank = dot(named.astype(BF), earlier.astype(F32).astype(BF))
    rank = jnp.where(named > 0, rank, -1.0)
    rank = jnp.broadcast_to(rank[:, None, :], (NE, 8, TOK)).reshape(NE * 8, TOK)
    weights = jnp.broadcast_to(weight[:, None, :], (NE, 8, TOK)).reshape(NE * 8, TOK)
    row = lax.broadcasted_iota(jnp.int32, (NE * 8, TOK), 0) & 7
    pick1 = rank == row.astype(F32)
    pick1_ref[...] = jnp.where(pick1, 1.0, 0.0).astype(BF)
    base = rank == (WHOLE + (row & 3)).astype(F32)
    left = base & (row < 4)
    right = base & (row >= 4)
    pick2_ref[:, :TOK] = jnp.where(left, 1.0, 0.0).astype(BF)
    pick2_ref[:, TOK:] = jnp.where(right, 1.0, 0.0).astype(BF)

    def put(ref, first, chosen):
        mix = jnp.transpose(jnp.where(chosen, weights, 0.0))
        high = mix.astype(BF)
        ref[first : first + TOK, :] = high
        ref[first + TOK : first + 2 * TOK, :] = (mix - high.astype(F32)).astype(BF)

    put(mix1_ref, 0, pick1)
    put(mix2_ref, 0, left)
    put(mix2_ref, 2 * TOK, right)
    stat_ref[...] = jnp.zeros((8, NE), F32)
    stat_ref[0:1, :] = jnp.sum(jnp.transpose(named), axis=0, keepdims=True)
    total = jnp.sum(jnp.transpose(weight), axis=0, keepdims=True)
    high = total.astype(BF).astype(F32)
    stat_ref[1:2, :] = high
    stat_ref[2:3, :] = total - high


def route_plan(routes, gates):
    return pl.pallas_call(
        route_kernel,
        out_shape=(
            pltpu.HBM((NE * 8, TOK), BF),
            pltpu.HBM((NE * 8, 2 * TOK), BF),
            pltpu.HBM((2 * TOK, NE * 8), BF),
            pltpu.HBM((4 * TOK, NE * 8), BF),
            pltpu.HBM((8, NE), F32),
        ),
        in_specs=[VM] * 2,
        out_specs=(VM,) * 5,
        compiler_params=params(8),
        name="route_plan",
    )(routes.T, gates.T)


def send_kernel(place_ref, q_ref, keys_ref, values_ref, weight_ref, *refs):
    out_refs, weight_out, sems = refs[:4], refs[4], refs[5]
    wide = GH * DH
    copies = []

    def fetch(source, target):
        copies.append(pltpu.make_async_copy(source, target, sems.at[len(copies)]))
        copies[-1].start()

    for step, out_ref in enumerate(out_refs):
        group = (place_ref[1] + step) % 4
        cols = pl.ds(pl.multiple_of(group * DH, DH), DH)
        fetch(q_ref.at[:, pl.ds(pl.multiple_of(group * wide, wide), wide)], out_ref.at[:, :wide])
        fetch(keys_ref.at[:, cols], out_ref.at[:, wide : wide + DH])
        fetch(values_ref.at[:, cols], out_ref.at[:, wide + DH :])
    rows = pl.ds(pl.multiple_of(place_ref[0] * QUARTER, QUARTER), QUARTER)
    fetch(weight_ref.at[rows], weight_out)
    for copy in copies:
        copy.wait()


def send_all(place, queries, keys, values, weight):
    return pl.pallas_call(
        send_kernel,
        out_shape=[pltpu.VMEM((TOK, SENT), BF)] * 4 + [pltpu.VMEM((QUARTER, D), BF)],
        in_specs=[SM] + [ANY] * 4,
        out_specs=[VM] * 5,
        scratch_shapes=[pltpu.SemaphoreType.DMA((13,))],
        compiler_params=params(4),
        name="send_all",
    )(place, *(far_memory(x) for x in (queries, keys, values, weight)))


def own_keys_kernel(place_ref, *refs):
    for step in range(4):
        refs[4][(place_ref[1] + 4 - step) % 4] = refs[step][:, GH * DH :]


def own_keys(place, blocks):
    return pl.pallas_call(
        own_keys_kernel,
        out_shape=pltpu.VMEM((4, TOK, 2 * DH), BF),
        in_specs=[SM] + [VM] * 4,
        out_specs=VM,
        compiler_params=params(4),
        name="own_keys",
    )(place, *(near_core(x) for x in blocks))


def later_kernel(x_ref, after_ref, out_ref):
    del x_ref, after_ref, out_ref


def later(x, after):
    return pl.pallas_call(
        later_kernel,
        out_shape=jax.ShapeDtypeStruct(x.shape, x.dtype),
        in_specs=[ANY, ANY],
        out_specs=ANY,
        input_output_aliases={0: 0},
        compiler_params=params(4),
        name="later",
    )(x, after)


def attend_kernel(place_ref, zero_ref, one_ref, two_ref, three_ref, own_ref, partner_ref, out_ref, q_ref):
    half = place_ref[2]
    first = pl.ds(pl.multiple_of(half * HALF, HALF), HALF)
    second = pl.ds(pl.multiple_of((1 - half) * HALF, HALF), HALF)
    for step, ref in enumerate((zero_ref, one_ref, two_ref, three_ref)):
        at = (place_ref[1] + 4 - step) % 4
        q_ref[at, :, :HALF] = ref[:, first]
        q_ref[at, :, HALF:] = ref[:, second]
    ones = jnp.ones((4 * TOK, DH), BF)
    sides = [ref[...].reshape(4 * TOK, 2 * DH) for ref in (own_ref, partner_ref)]
    keys = [side[:, :DH] for side in sides]
    values = [jnp.concatenate([side[:, DH:], ones], axis=1) for side in sides]
    scale = math.log2(math.e) / math.sqrt(DH)
    below = lax.broadcasted_iota(jnp.int32, (TOK, TOK), 1) <= lax.broadcasted_iota(
        jnp.int32, (TOK, TOK), 0
    )
    for block in range(4):
        upto = (block + 1) * TOK
        for head in range(GH):
            q = q_ref[block, :, head * DH : (head + 1) * DH]
            scores = []
            for side in range(2):
                score = lax.dot_general(
                    q, keys[side][:upto], (((1,), (1,)), ((), ())), preferred_element_type=F32
                )
                seen = below if side == 0 else jnp.full((TOK, TOK), half, jnp.int32) == 1
                last = jnp.where(seen, score[:, upto - TOK :], -jnp.inf)
                if block:
                    last = jnp.concatenate([score[:, : upto - TOK], last], axis=1)
                scores.append(last)
            top = jnp.maximum(
                jnp.max(scores[0], axis=1, keepdims=True), jnp.max(scores[1], axis=1, keepdims=True)
            )
            result = 0.0
            for side in range(2):
                expo = jnp.exp2((scores[side] - top) * scale).astype(BF)
                result = result + dot(expo, values[side][:upto])
            out_ref[block, :, head * DH : (head + 1) * DH] = (
                result[:, :DH] / result[:, DH:]
            ).astype(BF)


def attend(place, blocks, own, partner):
    return pl.pallas_call(
        attend_kernel,
        out_shape=pltpu.VMEM((4, TOK, GH * DH), BF),
        in_specs=[SM] + [VM] * 6,
        out_specs=VM,
        scratch_shapes=[pltpu.VMEM((4, TOK, GH * DH), BF)],
        compiler_params=params(16),
        cost_estimate=pl.CostEstimate(
            flops=2 * 2 * 512 * 8 * 640 * 128, bytes_accessed=3 << 20, transcendentals=512 * 8 * 640
        ),
        name="attend",
    )(place, *(near_core(x) for x in (*blocks, own, partner)))


def project_mine_kernel(heads_ref, mine_ref, out_ref):
    heads = heads_ref[:, :, :HALF].reshape(4 * TOK, HALF)
    cols = 512
    for j in range(0, D, cols):
        total = dot(heads, mine_ref[:, j : j + cols])
        out_ref[:, :, j : j + cols] = total.reshape(4, TOK, cols)


def project_mine(heads, mine):
    return pl.pallas_call(
        project_mine_kernel,
        out_shape=pltpu.VMEM((4, TOK, D), F32),
        in_specs=[VM] * 2,
        out_specs=VM,
        compiler_params=params(8),
        cost_estimate=pl.CostEstimate(
            flops=2 * 4 * TOK * HALF * D, bytes_accessed=8 << 20, transcendentals=0
        ),
        name="project_mine",
    )(near_core(heads), near_core(mine))


def project_kernel(steps, wanted, place_ref, heads_ref, mine_ref, near_ref, far_ref, *out_refs):
    core = place_ref[0]
    blocks = [(place_ref[1] + step) % 4 for step in steps]
    near = pl.multiple_of(HALF + core * QUARTER, QUARTER)
    far = pl.multiple_of(HALF + (1 - core) * QUARTER, QUARTER)

    def heads(first):
        rows = [heads_ref[block, :, pl.ds(first, QUARTER)] for block in blocks]
        return rows[0] if len(rows) == 1 else jnp.concatenate(rows, axis=0)

    second, third = heads(near), heads(far)
    cols = 512
    for j in range(0, D, cols):
        total = dot(second, near_ref[:, j : j + cols]) + dot(third, far_ref[:, j : j + cols])
        for (i, low, high, kind), out_ref in zip(wanted, out_refs):
            if low <= j < high:
                out = total[i * TOK : (i + 1) * TOK] + mine_ref[blocks[i], :, j : j + cols]
                out_ref[:, j - low : j - low + cols] = out.astype(kind)


def project(steps, wanted, place, heads, mine, near, far):
    return pl.pallas_call(
        functools.partial(project_kernel, steps, wanted),
        out_shape=[pltpu.VMEM((TOK, high - low), kind) for _, low, high, kind in wanted],
        in_specs=[SM] + [VM] * 4,
        out_specs=[VM] * len(wanted),
        compiler_params=params(8),
        cost_estimate=pl.CostEstimate(
            flops=2 * len(steps) * TOK * HALF * D, bytes_accessed=8 << 20, transcendentals=0
        ),
        name="project",
    )(place, near_core(heads), near_core(mine), near_core(near), near_core(far))


def join_kernel(a_ref, b_ref, c_ref, d_ref, left_ref, right_ref):
    left_ref[...] = (a_ref[...] + b_ref[...].astype(F32)).astype(BF)
    right_ref[...] = (c_ref[...] + d_ref[...].astype(F32)).astype(BF)


def join(*parts):
    return pl.pallas_call(
        join_kernel,
        out_shape=[pltpu.VMEM((TOK, D // 2), BF)] * 2,
        in_specs=[VM] * 4,
        out_specs=[VM] * 2,
        compiler_params=params(4),
        name="join",
    )(*(near_core(x) for x in parts))


def sum_over_z(place, heads, mine, near, far):
    half = D // 2
    operands = (place, heads, mine, near, far)
    left, right = project((2,), ((0, 0, half, BF), (0, half, D, BF)), *operands)
    left, right = turn(left, 1), turn(right, 3)
    wanted = ((0, half, D, BF), (1, 0, half, BF), (0, 0, half, F32), (1, half, D, F32))
    up_right, down_left, up_left, down_right = project((1, 3), wanted, *operands)
    up_right, down_left = turn(up_right, 1), turn(down_left, 3)
    (own,) = project((0,), ((0, 0, D, F32),), *operands)
    up_left, down_right = join(up_left, left, down_right, right)
    return own, turn(up_left, 1), up_right, down_left, turn(down_right, 3)


def residual_kernel(
    own_ref, up_left_ref, up_right_ref, down_left_ref, down_right_ref, hidden_any, gain_ref, pick1_any, pick2_any,
    att_ref, x_ref, hidden_ref, pick1_ref, pick2_ref, sems
):
    pairs = ((hidden_any, hidden_ref), (pick1_any, pick1_ref), (pick2_any, pick2_ref))
    copies = [pltpu.make_async_copy(a, b, sems.at[i]) for i, (a, b) in enumerate(pairs)]
    for copy in copies:
        copy.start()
    left = up_left_ref[...].astype(F32) + down_left_ref[...].astype(F32)
    right = up_right_ref[...].astype(F32) + down_right_ref[...].astype(F32)
    total = own_ref[...] + jnp.concatenate([left, right], axis=1)
    copies[0].wait()
    total = total + hidden_ref[...].astype(F32)
    att_ref[...] = total.astype(BF)
    square = jnp.mean(total * total, axis=1, keepdims=True)
    normed = (total / jnp.sqrt(square + 1e-06) * gain_ref[...]).astype(BF)
    stack = jnp.concatenate([normed[:, : D // 2], normed[:, D // 2 :]], axis=0)
    copies[1].wait()
    copies[2].wait()
    rows = 256
    for first in range(0, NE * 8, rows):
        x_ref[first : first + rows, :D] = dot(pick1_ref[first : first + rows], normed).astype(BF)
        x_ref[first : first + rows, D:] = dot(pick2_ref[first : first + rows], stack).astype(BF)


def residual(sums, hidden, gain, pick1, pick2):
    return pl.pallas_call(
        residual_kernel,
        out_shape=(jax.ShapeDtypeStruct((TOK, D), BF), pltpu.VMEM((NE * 8, WIDE), BF)),
        in_specs=[VM] * 5 + [ANY, VM, ANY, ANY],
        out_specs=(VM, VM),
        scratch_shapes=[
            pltpu.VMEM(hidden.shape, BF),
            pltpu.VMEM(pick1.shape, BF),
            pltpu.VMEM(pick2.shape, BF),
            pltpu.SemaphoreType.DMA((3,)),
        ],
        compiler_params=params(12),
        cost_estimate=pl.CostEstimate(flops=1 << 30, bytes_accessed=10 << 20, transcendentals=128),
        name="residual_norm_pick",
    )(
        *(near_core(x) for x in sums),
        far_memory(hidden),
        gain.reshape(1, D),
        far_memory(pick1),
        far_memory(pick2),
    )


def expert_kernel(x_ref, gate_ref, up_ref, down_ref, stat_ref, y_ref):
    rows = 512
    piece = 256
    count = piece // 2
    half = D // 2
    to = lax.broadcasted_iota(jnp.int32, (piece, piece), 0)
    at = lax.broadcasted_iota(jnp.int32, (piece, piece), 1)

    def source(i):
        side = (i >= count).astype(jnp.int32)
        own = i - side * count
        return (own >> 2) * 8 + side * 4 + (own & 3)

    sort = jnp.where(source(to) == at, 1.0, 0.0).astype(BF)
    back = jnp.where(source(at) == to, 1.0, 0.0).astype(BF)
    stat = jnp.broadcast_to(stat_ref[...][None], (rows // 8, 8, NE)).reshape(rows, NE).astype(BF)

    def step(i, carry):
        base = i * rows
        span = pl.ds(pl.multiple_of(base, rows), rows)
        pieces = [pl.ds(pl.multiple_of(base + p, piece), piece) for p in range(0, rows, piece)]
        parts = [x_ref[span, :D]]
        for at in pieces:
            rest = dot(sort, x_ref[at, D:]).astype(BF)
            parts.append(jnp.concatenate([rest[:count], rest[count:]], axis=1))
        x = jnp.concatenate(parts, axis=0)
        gate = dot(x, gate_ref[0])
        hidden = (gate / (1.0 + jnp.exp(-gate)) * dot(x, up_ref[0])).astype(BF)
        y = dot(hidden, down_ref[0]).astype(BF)
        y_ref[span, :D] = y[:rows]
        for p, at in enumerate(pieces):
            rest = y[rows + p * count : rows + (p + 1) * count]
            rest = jnp.concatenate([rest[:, :half], rest[:, half:]], axis=0)
            y_ref[at, D:WIDE] = dot(back, rest).astype(BF)
        y_ref[span, WIDE:] = stat
        return carry

    lax.fori_loop(0, NE * 8 // rows, step, 0)


def expert_apply(x, w_gate, w_up, w_down, stat):
    return pl.pallas_call(
        expert_kernel,
        out_shape=pltpu.VMEM((NE * 8, WIDE + NE), BF),
        in_specs=[VM] * 5,
        out_specs=VM,
        compiler_params=params(16),
        cost_estimate=pl.CostEstimate(
            flops=6 * NE * CAP * D * FF, bytes_accessed=22 << 20, transcendentals=NE * CAP * FF
        ),
        name="experts",
    )(near_core(x), near_core(w_gate), near_core(w_up), near_core(w_down), near_core(stat))


def mix_kernel(mix1_ref, mix2_ref, y_ref, out_ref, load_ref, loss_ref):
    cols = 512
    for j in range(D // cols):
        at = j * cols
        side = (j // 2) * 2 * TOK
        rest = D + (j % 2) * cols
        both = dot(mix1_ref[...], y_ref[:, at : at + cols])
        both = both + dot(mix2_ref[side : side + 2 * TOK], y_ref[:, rest : rest + cols])
        out_ref[:, at : at + cols] = (both[:TOK] + both[TOK:]).astype(BF)
    stat = jnp.sum(y_ref[:, WIDE:].astype(F32).reshape(NE, 8, NE), axis=0)
    counts = stat[0:1]
    gates = stat[1:2] + stat[2:3]
    tokens = TOK * NE
    load = counts / (tokens * TOP)
    load_ref[...] = NE * load
    loss = NE * jnp.sum(load * (gates / tokens), axis=1, keepdims=True)
    loss_ref[...] = jnp.broadcast_to(loss, (1, NE))


def mix(mix1, mix2, y):
    return pl.pallas_call(
        mix_kernel,
        out_shape=(
            jax.ShapeDtypeStruct((TOK, D), BF),
            jax.ShapeDtypeStruct((1, NE), F32),
            jax.ShapeDtypeStruct((1, NE), F32),
        ),
        in_specs=[VM] * 3,
        out_specs=(VM,) * 3,
        compiler_params=params(12),
        cost_estimate=pl.CostEstimate(flops=2 << 30, bytes_accessed=8 << 20, transcendentals=0),
        name="mix",
    )(near_core(mix1), near_core(mix2), near_core(y))


def swap(x, axis, count, step):
    return lax.ppermute(x, axis, [(i, i ^ step) for i in range(count)])


def turn(x, step):
    return lax.ppermute(x, "ctx", [(i, (i + 2 * step) % CTX) for i in range(CTX)])


def exchange(x):
    return lax.all_to_all(x, ALL, split_axis=0, concat_axis=0, tiled=True)


def on_device(
    hidden_in, queries, keys, values, out_weight, norm_gain, routes, gates, w_gate, w_up, w_down
):
    spot = lax.axis_index("ctx").astype(jnp.int32)
    core = lax.axis_index("dp").astype(jnp.int32) % 2
    place = jnp.stack([core, spot // 2, spot % 2])
    *blocks, weight = send_all(place, queries, keys, values, out_weight)
    near = swap(weight, "ctx", CTX, 1)
    blocks = [blocks[0]] + [turn(blocks[step], step) for step in (1, 2, 3)]
    own = own_keys(place, blocks)
    partner = swap(own, "ctx", CTX, 1)
    near = later(near, partner)
    far = swap(near, "dp", 16, 1)
    pick1, pick2, mix1, mix2, stat = route_plan(routes, gates)
    heads = attend(place, blocks, own, partner)
    mine = project_mine(heads, out_weight)
    sums = sum_over_z(place, heads, mine, near, far)
    attended, x = residual(sums, hidden_in, norm_gain, pick1, pick2)
    x = exchange(x.reshape(NE, 8, WIDE))
    y = expert_apply(x.reshape(NE * 8, WIDE), w_gate, w_up, w_down, stat)
    y = exchange(y.reshape(NE, 8, WIDE + NE))
    expert_mix, load, loss = mix(mix1, mix2, y.reshape(NE * 8, WIDE + NE))
    return attended, expert_mix, loss[0, 0], load[0]


def solution(mesh):
    rows = P(ALL, None)
    return jax.shard_map(
        on_device,
        mesh=mesh,
        in_specs=(
            rows,
            rows,
            rows,
            rows,
            P("ctx", None),
            P(),
            rows,
            rows,
            P(ALL, None, None),
            P(ALL, None, None),
            P(ALL, None, None),
        ),
        out_specs=(rows, rows, P(), P()),
        check_vma=False,
    )
```

```python
import functools
import math

import jax
import jax.numpy as jnp
from jax import lax
from jax.experimental import pallas as pl
from jax.experimental.pallas import tpu as pltpu
from jax.sharding import PartitionSpec as P

H = 32
KV = 4
DH = 128
TOP = 8
D = 2048
FF = 768
TOK = 128
NE = 128
CTX = 8
GH = H // KV
HALF = 512
WHOLE = 8
CAP = 12
PIECE = 128
WIDE = 3072
ALL = ("dp", "ctx")
BF = jnp.bfloat16
F32 = jnp.float32
def params(megabytes):
    return pltpu.CompilerParams(vmem_limit_bytes=megabytes << 20)


def near_core(x):
    return pltpu.with_memory_space_constraint(x, pltpu.VMEM)


def far_memory(x):
    return pltpu.with_memory_space_constraint(x, pltpu.HBM)


ANY = pl.BlockSpec(memory_space=pl.ANY)
VM = pl.BlockSpec(memory_space=pltpu.VMEM)
SM = pl.BlockSpec(memory_space=pltpu.SMEM)


def dot(a, b):
    return jnp.dot(a, b, preferred_element_type=F32)


def route_kernel(routes_ref, gates_ref, pick1_ref, pick2_ref, mix1_ref, mix2_ref, stat_ref):
    experts = lax.broadcasted_iota(jnp.int32, (NE, TOK), 0)
    named = jnp.zeros((NE, TOK), F32)
    weight = jnp.zeros((NE, TOK), F32)
    for k in range(TOP):
        hit = routes_ref[k : k + 1, :] == experts
        named = jnp.where(hit, 1.0, named)
        weight = jnp.where(hit, gates_ref[k : k + 1, :], weight)
    earlier = lax.broadcasted_iota(jnp.int32, (TOK, TOK), 0) < lax.broadcasted_iota(
        jnp.int32, (TOK, TOK), 1
    )
    rank = dot(named.astype(BF), earlier.astype(F32).astype(BF))
    rank = jnp.where(named > 0, rank, -1.0)
    rank = jnp.broadcast_to(rank[:, None, :], (NE, 8, TOK)).reshape(NE * 8, TOK)
    weights = jnp.broadcast_to(weight[:, None, :], (NE, 8, TOK)).reshape(NE * 8, TOK)
    row = lax.broadcasted_iota(jnp.int32, (NE * 8, TOK), 0) & 7
    pick1 = rank == row.astype(F32)
    pick1_ref[...] = jnp.where(pick1, 1.0, 0.0).astype(BF)
    base = rank == (WHOLE + (row & 3)).astype(F32)
    left = base & (row < 4)
    right = base & (row >= 4)
    pick2_ref[:, :TOK] = jnp.where(left, 1.0, 0.0).astype(BF)
    pick2_ref[:, TOK:] = jnp.where(right, 1.0, 0.0).astype(BF)

    def put(ref, first, chosen):
        mix = jnp.transpose(jnp.where(chosen, weights, 0.0))
        high = mix.astype(BF)
        ref[first : first + TOK, :] = high
        ref[first + TOK : first + 2 * TOK, :] = (mix - high.astype(F32)).astype(BF)

    put(mix1_ref, 0, pick1)
    put(mix2_ref, 0, left)
    put(mix2_ref, 2 * TOK, right)
    stat_ref[...] = jnp.zeros((8, NE), F32)
    stat_ref[0:1, :] = jnp.sum(jnp.transpose(named), axis=0, keepdims=True)
    total = jnp.sum(jnp.transpose(weight), axis=0, keepdims=True)
    high = total.astype(BF).astype(F32)
    stat_ref[1:2, :] = high
    stat_ref[2:3, :] = total - high


def route_plan(routes, gates):
    return pl.pallas_call(
        route_kernel,
        out_shape=(
            pltpu.HBM((NE * 8, TOK), BF),
            pltpu.HBM((NE * 8, 2 * TOK), BF),
            pltpu.HBM((2 * TOK, NE * 8), BF),
            pltpu.HBM((4 * TOK, NE * 8), BF),
            pltpu.HBM((8, NE), F32),
        ),
        in_specs=[VM] * 2,
        out_specs=(VM,) * 5,
        compiler_params=params(8),
        name="route_plan",
    )(routes.T, gates.T)


def fetch_all(pairs, sems):
    copies = [pltpu.make_async_copy(a, b, sems.at[i]) for i, (a, b) in enumerate(pairs)]
    for copy in copies:
        copy.start()
    for copy in copies:
        copy.wait()


def group_cols(place_ref, step, size):
    group = (place_ref[1] + step) % 4
    return pl.ds(pl.multiple_of(group * size, size), size)


def send_kernel(place_ref, keys_ref, values_ref, q_ref, weight_ref, *refs):
    rows = pl.ds(pl.multiple_of((2 * place_ref[0] + place_ref[3]) * PIECE, PIECE), PIECE)
    pairs = [(weight_ref.at[rows], refs[8])]
    for step in range(4):
        cols = group_cols(place_ref, step, DH)
        pairs.append((keys_ref.at[:, cols], refs[step].at[:, :DH]))
        pairs.append((values_ref.at[:, cols], refs[step].at[:, DH:]))
        pairs.append((q_ref.at[:, group_cols(place_ref, step, GH * DH)], refs[4 + step]))
    fetch_all(pairs, refs[9])


def send_all(place, *arrays):
    return pl.pallas_call(
        send_kernel,
        out_shape=[pltpu.VMEM((TOK, 2 * DH), BF)] * 4
        + [pltpu.VMEM((TOK, GH * DH), BF)] * 4
        + [pltpu.VMEM((PIECE, D), BF)],
        in_specs=[SM] + [ANY] * 4,
        out_specs=[VM] * 9,
        scratch_shapes=[pltpu.SemaphoreType.DMA((13,))],
        compiler_params=params(4),
        name="send_all",
    )(place, *(far_memory(x) for x in arrays))


def own_keys_kernel(place_ref, *refs):
    for step in range(4):
        refs[5][(place_ref[1] + 4 - step) % 4] = refs[step][...]


def own_keys(place, blocks, after):
    return pl.pallas_call(
        own_keys_kernel,
        out_shape=pltpu.VMEM((4, TOK, 2 * DH), BF),
        in_specs=[SM] + [VM] * 4 + [ANY],
        out_specs=VM,
        compiler_params=params(4),
        name="own_keys",
    )(place, *(near_core(x) for x in blocks), after)


def later_kernel(x_ref, after_ref, out_ref):
    del x_ref, after_ref, out_ref


def later(x, after):
    return pl.pallas_call(
        later_kernel,
        out_shape=jax.ShapeDtypeStruct(x.shape, x.dtype),
        in_specs=[ANY, ANY],
        out_specs=ANY,
        input_output_aliases={0: 0},
        compiler_params=params(4),
        name="later",
    )(x, after)


SCALE = math.log2(math.e) / math.sqrt(DH)


def scores_of(q, keys):
    return lax.dot_general(q, keys, (((1,), (1,)), ((), ())), preferred_element_type=F32)


def with_ones(values):
    return jnp.concatenate([values, jnp.ones(values.shape, BF)], axis=1)


def attend_kernel(place_ref, zero_ref, one_ref, two_ref, three_ref, own_ref, partner_ref, out_ref, q_ref):
    core, half, turned = place_ref[0], place_ref[2], place_ref[3]
    firsts = [half * HALF + i * DH for i in range(GH // 2)]
    for c in (core, 1 - core):
        for y in (turned, 1 - turned):
            firsts.append((1 - half) * HALF + (2 * c + y) * DH)
    for step, ref in enumerate((zero_ref, one_ref, two_ref, three_ref)):
        at = (place_ref[1] + 4 - step) % 4
        for head, first in enumerate(firsts):
            q_ref[at, head * TOK : (head + 1) * TOK, :] = ref[:, pl.ds(pl.multiple_of(first, DH), DH)]
    sides = [ref[...].reshape(4 * TOK, 2 * DH) for ref in (own_ref, partner_ref)]
    keys = [side[:, :DH] for side in sides]
    values = [with_ones(side[:, DH:]) for side in sides]
    heads = 4
    rows = heads * TOK
    own_row = lax.broadcasted_iota(jnp.int32, (rows, TOK), 0) & (TOK - 1)
    below = lax.broadcasted_iota(jnp.int32, (rows, TOK), 1) <= own_row
    shown = jnp.full((rows, TOK), half, jnp.int32) == 1
    for block in range(4):
        upto = (block + 1) * TOK
        before = upto - TOK
        key = jnp.concatenate([k[:upto] for k in keys], axis=0)
        value = jnp.concatenate([v[:upto] for v in values], axis=0)
        for head in range(0, GH, heads):
            q = q_ref[block, head * TOK : (head + heads) * TOK, :]
            score = scores_of(q, key)
            parts = []
            for side, seen in enumerate((below, shown)):
                if block:
                    parts.append(score[:, side * upto : side * upto + before])
                last = score[:, side * upto + before : (side + 1) * upto]
                parts.append(jnp.where(seen, last, -jnp.inf))
            score = jnp.concatenate(parts, axis=1)
            top = jnp.max(score, axis=1, keepdims=True)
            result = dot(jnp.exp2((score - top) * SCALE).astype(BF), value)
            result = (result[:, :DH] / result[:, DH:]).astype(BF)
            for i in range(heads):
                cols = slice((head + i) * DH, (head + i + 1) * DH)
                out_ref[block, :, cols] = result[i * TOK : (i + 1) * TOK]


def attend(place, blocks, own, partner):
    return pl.pallas_call(
        attend_kernel,
        out_shape=pltpu.VMEM((4, TOK, GH * DH), BF),
        in_specs=[SM] + [VM] * 6,
        out_specs=VM,
        scratch_shapes=[pltpu.VMEM((4, GH * TOK, DH), BF)],
        compiler_params=params(16),
        cost_estimate=pl.CostEstimate(
            flops=5 << 30, bytes_accessed=8 << 20, transcendentals=512 * 8 * 640
        ),
        name="attend",
    )(place, *(near_core(x) for x in (*blocks, own, partner)))


def project_mine_kernel(heads_ref, mine_ref, out_ref):
    heads = heads_ref[:, :, :HALF].reshape(4 * TOK, HALF)
    cols = 512
    for j in range(0, D, cols):
        total = dot(heads, mine_ref[:, j : j + cols])
        out_ref[:, :, j : j + cols] = total.reshape(4, TOK, cols)


def project_mine(heads, mine):
    return pl.pallas_call(
        project_mine_kernel,
        out_shape=pltpu.VMEM((4, TOK, D), F32),
        in_specs=[VM] * 2,
        out_specs=VM,
        compiler_params=params(8),
        cost_estimate=pl.CostEstimate(
            flops=2 * 4 * TOK * HALF * D, bytes_accessed=8 << 20, transcendentals=0
        ),
        name="project_mine",
    )(near_core(heads), near_core(mine))


def project_kernel(steps, wanted, place_ref, heads_ref, mine_ref, *refs):
    others, out_refs = refs[:4], refs[4:]
    blocks = [(place_ref[1] + step) % 4 for step in steps]
    rows = [heads_ref[block, :, HALF:] for block in blocks]
    heads = rows[0] if len(rows) == 1 else jnp.concatenate(rows, axis=0)
    cols = 512
    for j in range(0, D, cols):
        other = jnp.concatenate([ref[:, j : j + cols] for ref in others], axis=0)
        total = dot(heads, other)
        for (i, low, high, kind), out_ref in zip(wanted, out_refs):
            if low <= j < high:
                out = total[i * TOK : (i + 1) * TOK] + mine_ref[blocks[i], :, j : j + cols]
                out_ref[:, j - low : j - low + cols] = out.astype(kind)


def project(steps, wanted, place, *arrays):
    return pl.pallas_call(
        functools.partial(project_kernel, steps, wanted),
        out_shape=[pltpu.VMEM((TOK, high - low), kind) for _, low, high, kind in wanted],
        in_specs=[SM] + [VM] * 6,
        out_specs=[VM] * len(wanted),
        compiler_params=params(12),
        cost_estimate=pl.CostEstimate(
            flops=2 * len(steps) * TOK * 2 * HALF * D, bytes_accessed=8 << 20, transcendentals=0
        ),
        name="project",
    )(place, *(near_core(x) for x in arrays))


def join_kernel(a_ref, b_ref, c_ref, d_ref, left_ref, right_ref):
    left_ref[...] = (a_ref[...] + b_ref[...].astype(F32)).astype(BF)
    right_ref[...] = (c_ref[...] + d_ref[...].astype(F32)).astype(BF)


def join(*parts):
    return pl.pallas_call(
        join_kernel,
        out_shape=[pltpu.VMEM((TOK, D // 2), BF)] * 2,
        in_specs=[VM] * 4,
        out_specs=[VM] * 2,
        compiler_params=params(4),
        name="join",
    )(*(near_core(x) for x in parts))


def sum_over_z(*operands):
    half = D // 2
    left, right = project((2,), ((0, 0, half, BF), (0, half, D, BF)), *operands)
    left, right = turn(left, 1), turn(right, 3)
    wanted = ((0, half, D, BF), (1, 0, half, BF), (0, 0, half, F32), (1, half, D, F32))
    up_right, down_left, up_left, down_right = project((1, 3), wanted, *operands)
    up_right, down_left = turn(up_right, 1), turn(down_left, 3)
    (own,) = project((0,), ((0, 0, D, F32),), *operands)
    up_left, down_right = join(up_left, left, down_right, right)
    return own, turn(up_left, 1), up_right, down_left, turn(down_right, 3)


def residual_kernel(
    own_ref, up_left_ref, up_right_ref, down_left_ref, down_right_ref, hidden_any, gain_ref, pick1_any, pick2_any,
    att_ref, x_ref, hidden_ref, pick1_ref, pick2_ref, sems
):
    pairs = ((hidden_any, hidden_ref), (pick1_any, pick1_ref), (pick2_any, pick2_ref))
    copies = [pltpu.make_async_copy(a, b, sems.at[i]) for i, (a, b) in enumerate(pairs)]
    for copy in copies:
        copy.start()
    left = up_left_ref[...].astype(F32) + down_left_ref[...].astype(F32)
    right = up_right_ref[...].astype(F32) + down_right_ref[...].astype(F32)
    total = own_ref[...] + jnp.concatenate([left, right], axis=1)
    copies[0].wait()
    total = total + hidden_ref[...].astype(F32)
    att_ref[...] = total.astype(BF)
    square = jnp.mean(total * total, axis=1, keepdims=True)
    normed = (total / jnp.sqrt(square + 1e-06) * gain_ref[...]).astype(BF)
    stack = jnp.concatenate([normed[:, : D // 2], normed[:, D // 2 :]], axis=0)
    copies[1].wait()
    copies[2].wait()
    rows = 256
    for first in range(0, NE * 8, rows):
        x_ref[first : first + rows, :D] = dot(pick1_ref[first : first + rows], normed).astype(BF)
        x_ref[first : first + rows, D:] = dot(pick2_ref[first : first + rows], stack).astype(BF)


def residual(sums, hidden, gain, pick1, pick2):
    return pl.pallas_call(
        residual_kernel,
        out_shape=(jax.ShapeDtypeStruct((TOK, D), BF), pltpu.VMEM((NE * 8, WIDE), BF)),
        in_specs=[VM] * 5 + [ANY, VM, ANY, ANY],
        out_specs=(VM, VM),
        scratch_shapes=[
            pltpu.VMEM(hidden.shape, BF),
            pltpu.VMEM(pick1.shape, BF),
            pltpu.VMEM(pick2.shape, BF),
            pltpu.SemaphoreType.DMA((3,)),
        ],
        compiler_params=params(12),
        cost_estimate=pl.CostEstimate(flops=1 << 30, bytes_accessed=10 << 20, transcendentals=128),
        name="residual_norm_pick",
    )(
        *(near_core(x) for x in sums),
        far_memory(hidden),
        gain.reshape(1, D),
        far_memory(pick1),
        far_memory(pick2),
    )


def expert_kernel(x_ref, gate_ref, up_ref, down_ref, stat_ref, y_ref):
    rows = 512
    piece = 256
    count = piece // 2
    half = D // 2
    to = lax.broadcasted_iota(jnp.int32, (piece, piece), 0)
    at = lax.broadcasted_iota(jnp.int32, (piece, piece), 1)

    def source(i):
        side = (i >= count).astype(jnp.int32)
        own = i - side * count
        return (own >> 2) * 8 + side * 4 + (own & 3)

    sort = jnp.where(source(to) == at, 1.0, 0.0).astype(BF)
    back = jnp.where(source(at) == to, 1.0, 0.0).astype(BF)
    stat = jnp.broadcast_to(stat_ref[...][None], (rows // 8, 8, NE)).reshape(rows, NE).astype(BF)

    def step(i, carry):
        base = i * rows
        span = pl.ds(pl.multiple_of(base, rows), rows)
        pieces = [pl.ds(pl.multiple_of(base + p, piece), piece) for p in range(0, rows, piece)]
        parts = [x_ref[span, :D]]
        for at in pieces:
            rest = dot(sort, x_ref[at, D:]).astype(BF)
            parts.append(jnp.concatenate([rest[:count], rest[count:]], axis=1))
        x = jnp.concatenate(parts, axis=0)
        gate = dot(x, gate_ref[0])
        hidden = (gate / (1.0 + jnp.exp(-gate)) * dot(x, up_ref[0])).astype(BF)
        y = dot(hidden, down_ref[0]).astype(BF)
        y_ref[span, :D] = y[:rows]
        for p, at in enumerate(pieces):
            rest = y[rows + p * count : rows + (p + 1) * count]
            rest = jnp.concatenate([rest[:, :half], rest[:, half:]], axis=0)
            y_ref[at, D:WIDE] = dot(back, rest).astype(BF)
        y_ref[span, WIDE:] = stat
        return carry

    lax.fori_loop(0, NE * 8 // rows, step, 0)


def expert_apply(x, w_gate, w_up, w_down, stat):
    return pl.pallas_call(
        expert_kernel,
        out_shape=pltpu.VMEM((NE * 8, WIDE + NE), BF),
        in_specs=[VM] * 5,
        out_specs=VM,
        compiler_params=params(16),
        cost_estimate=pl.CostEstimate(
            flops=6 * NE * CAP * D * FF, bytes_accessed=22 << 20, transcendentals=NE * CAP * FF
        ),
        name="experts",
    )(near_core(x), near_core(w_gate), near_core(w_up), near_core(w_down), near_core(stat))


def mix_kernel(mix1_ref, mix2_ref, y_ref, out_ref, load_ref, loss_ref):
    cols = 512
    for j in range(D // cols):
        at = j * cols
        side = (j // 2) * 2 * TOK
        rest = D + (j % 2) * cols
        both = dot(mix1_ref[...], y_ref[:, at : at + cols])
        both = both + dot(mix2_ref[side : side + 2 * TOK], y_ref[:, rest : rest + cols])
        out_ref[:, at : at + cols] = (both[:TOK] + both[TOK:]).astype(BF)
    stat = jnp.sum(y_ref[:, WIDE:].astype(F32).reshape(NE, 8, NE), axis=0)
    counts = stat[0:1]
    gates = stat[1:2] + stat[2:3]
    tokens = TOK * NE
    load = counts / (tokens * TOP)
    load_ref[...] = NE * load
    loss = NE * jnp.sum(load * (gates / tokens), axis=1, keepdims=True)
    loss_ref[...] = jnp.broadcast_to(loss, (1, NE))


def mix(mix1, mix2, y):
    return pl.pallas_call(
        mix_kernel,
        out_shape=(
            jax.ShapeDtypeStruct((TOK, D), BF),
            jax.ShapeDtypeStruct((1, NE), F32),
            jax.ShapeDtypeStruct((1, NE), F32),
        ),
        in_specs=[VM] * 3,
        out_specs=(VM,) * 3,
        compiler_params=params(12),
        cost_estimate=pl.CostEstimate(flops=2 << 30, bytes_accessed=8 << 20, transcendentals=0),
        name="mix",
    )(near_core(mix1), near_core(mix2), near_core(y))


def swap(x, axis, count, step):
    return lax.ppermute(x, axis, [(i, i ^ step) for i in range(count)])


def turn(x, step):
    return lax.ppermute(x, "ctx", [(i, (i + 2 * step) % CTX) for i in range(CTX)])


def turn_all(blocks):
    return [blocks[0]] + [turn(blocks[step], step) for step in (1, 2, 3)]


def exchange(x):
    return lax.all_to_all(x, ALL, split_axis=0, concat_axis=0, tiled=True)


def on_device(
    hidden_in, queries, keys, values, out_weight, norm_gain, routes, gates, w_gate, w_up, w_down
):
    spot = lax.axis_index("ctx").astype(jnp.int32)
    column = lax.axis_index("dp").astype(jnp.int32)
    place = jnp.stack([column % 2, spot // 2, spot % 2, column // 2 % 2])
    *sent, weight = send_all(place, keys, values, queries, out_weight)
    first = lax.ppermute(weight, ALL, [(i, i ^ 65) for i in range(NE)])
    sent, blocks = turn_all(sent[:4]), turn_all(sent[4:])
    own = own_keys(place, sent, blocks[2])
    partner = swap(own, "ctx", CTX, 1)
    first = later(first, own)
    second = swap(first, "dp", 16, 2)
    first, second = later(first, partner), later(second, partner)
    third, fourth = swap(first, "dp", 16, 1), swap(second, "dp", 16, 1)
    pick1, pick2, mix1, mix2, stat = route_plan(routes, gates)
    heads = attend(place, blocks, own, partner)
    mine = project_mine(heads, out_weight)
    sums = sum_over_z(place, heads, mine, first, second, third, fourth)
    attended, x = residual(sums, hidden_in, norm_gain, pick1, pick2)
    x = exchange(x.reshape(NE, 8, WIDE))
    y = expert_apply(x.reshape(NE * 8, WIDE), w_gate, w_up, w_down, stat)
    y = exchange(y.reshape(NE, 8, WIDE + NE))
    expert_mix, load, loss = mix(mix1, mix2, y.reshape(NE * 8, WIDE + NE))
    return attended, expert_mix, loss[0, 0], load[0]


def solution(mesh):
    rows = P(ALL, None)
    return jax.shard_map(
        on_device,
        mesh=mesh,
        in_specs=(
            rows,
            rows,
            rows,
            rows,
            P("ctx", None),
            P(),
            rows,
            rows,
            P(ALL, None, None),
            P(ALL, None, None),
            P(ALL, None, None),
        ),
        out_specs=(rows, rows, P(), P()),
        check_vma=False,
    )
```

```python
import functools
import math

import jax
import jax.numpy as jnp
from jax import lax
from jax.experimental import pallas as pl
from jax.experimental.pallas import tpu as pltpu
from jax.sharding import PartitionSpec as P

H = 32
KV = 4
DH = 128
TOP = 8
D = 2048
FF = 768
TOK = 128
NE = 128
CTX = 8
GH = H // KV
HALF = 512
WHOLE = 8
CAP = 12
PIECE = 128
WIDE = 3072
ALL = ("dp", "ctx")
BF = jnp.bfloat16
F32 = jnp.float32
def params(megabytes):
    return pltpu.CompilerParams(vmem_limit_bytes=megabytes << 20)


def near_core(x):
    return pltpu.with_memory_space_constraint(x, pltpu.VMEM)


def far_memory(x):
    return pltpu.with_memory_space_constraint(x, pltpu.HBM)


ANY = pl.BlockSpec(memory_space=pl.ANY)
VM = pl.BlockSpec(memory_space=pltpu.VMEM)
SM = pl.BlockSpec(memory_space=pltpu.SMEM)


def dot(a, b):
    return jnp.dot(a, b, preferred_element_type=F32)


def route_kernel(routes_ref, gates_ref, pick1_ref, pick2_ref, mix1_ref, mix2_ref, stat_ref):
    experts = lax.broadcasted_iota(jnp.int32, (NE, TOK), 0)
    named = jnp.zeros((NE, TOK), F32)
    weight = jnp.zeros((NE, TOK), F32)
    for k in range(TOP):
        hit = routes_ref[k : k + 1, :] == experts
        named = jnp.where(hit, 1.0, named)
        weight = jnp.where(hit, gates_ref[k : k + 1, :], weight)
    earlier = lax.broadcasted_iota(jnp.int32, (TOK, TOK), 0) < lax.broadcasted_iota(
        jnp.int32, (TOK, TOK), 1
    )
    rank = dot(named.astype(BF), earlier.astype(F32).astype(BF))
    rank = jnp.where(named > 0, rank, -1.0)
    rank = jnp.broadcast_to(rank[:, None, :], (NE, 8, TOK)).reshape(NE * 8, TOK)
    weights = jnp.broadcast_to(weight[:, None, :], (NE, 8, TOK)).reshape(NE * 8, TOK)
    row = lax.broadcasted_iota(jnp.int32, (NE * 8, TOK), 0) & 7
    pick1 = rank == row.astype(F32)
    pick1_ref[...] = jnp.where(pick1, 1.0, 0.0).astype(BF)
    base = rank == (WHOLE + (row & 3)).astype(F32)
    left = base & (row < 4)
    right = base & (row >= 4)
    pick2_ref[:, :TOK] = jnp.where(left, 1.0, 0.0).astype(BF)
    pick2_ref[:, TOK:] = jnp.where(right, 1.0, 0.0).astype(BF)

    def put(ref, first, chosen):
        mix = jnp.transpose(jnp.where(chosen, weights, 0.0))
        high = mix.astype(BF)
        ref[first : first + TOK, :] = high
        ref[first + TOK : first + 2 * TOK, :] = (mix - high.astype(F32)).astype(BF)

    put(mix1_ref, 0, pick1)
    put(mix2_ref, 0, left)
    put(mix2_ref, 2 * TOK, right)
    stat_ref[...] = jnp.zeros((8, NE), F32)
    stat_ref[0:1, :] = jnp.sum(jnp.transpose(named), axis=0, keepdims=True)
    total = jnp.sum(jnp.transpose(weight), axis=0, keepdims=True)
    high = total.astype(BF).astype(F32)
    stat_ref[1:2, :] = high
    stat_ref[2:3, :] = total - high


def route_plan(routes, gates):
    return pl.pallas_call(
        route_kernel,
        out_shape=(
            pltpu.VMEM((NE * 8, TOK), BF),
            pltpu.VMEM((NE * 8, 2 * TOK), BF),
            pltpu.HBM((2 * TOK, NE * 8), BF),
            pltpu.HBM((4 * TOK, NE * 8), BF),
            pltpu.HBM((8, NE), F32),
        ),
        in_specs=[VM] * 2,
        out_specs=(VM,) * 5,
        compiler_params=params(8),
        name="route_plan",
    )(routes.T, gates.T)


def fetch_all(pairs, sems):
    copies = [pltpu.make_async_copy(a, b, sems.at[i]) for i, (a, b) in enumerate(pairs)]
    for copy in copies:
        copy.start()
    for copy in copies:
        copy.wait()


def group_cols(place_ref, step, size):
    group = (place_ref[1] + step) % 4
    return pl.ds(pl.multiple_of(group * size, size), size)


def send_kernel(place_ref, keys_ref, values_ref, q_ref, weight_ref, *refs):
    rows = pl.ds(pl.multiple_of((2 * place_ref[0] + place_ref[3]) * PIECE, PIECE), PIECE)
    pairs = [(weight_ref.at[rows], refs[8])]
    for step in range(4):
        cols = group_cols(place_ref, step, DH)
        pairs.append((keys_ref.at[:, cols], refs[step].at[:, :DH]))
        pairs.append((values_ref.at[:, cols], refs[step].at[:, DH:]))
        pairs.append((q_ref.at[:, group_cols(place_ref, step, GH * DH)], refs[4 + step]))
    fetch_all(pairs, refs[9])


def send_all(place, *arrays):
    return pl.pallas_call(
        send_kernel,
        out_shape=[pltpu.VMEM((TOK, 2 * DH), BF)] * 4
        + [pltpu.VMEM((TOK, GH * DH), BF)] * 4
        + [pltpu.VMEM((PIECE, D), BF)],
        in_specs=[SM] + [ANY] * 4,
        out_specs=[VM] * 9,
        scratch_shapes=[pltpu.SemaphoreType.DMA((13,))],
        compiler_params=params(4),
        name="send_all",
    )(place, *(far_memory(x) for x in arrays))


def own_keys_kernel(place_ref, *refs):
    for step in range(4):
        refs[5][(place_ref[1] + 4 - step) % 4] = refs[step][...]


def own_keys(place, blocks, after):
    return pl.pallas_call(
        own_keys_kernel,
        out_shape=pltpu.VMEM((4, TOK, 2 * DH), BF),
        in_specs=[SM] + [VM] * 4 + [ANY],
        out_specs=VM,
        compiler_params=params(4),
        name="own_keys",
    )(place, *(near_core(x) for x in blocks), after)


def later_kernel(x_ref, after_ref, out_ref):
    del x_ref, after_ref, out_ref


def later(x, after):
    return pl.pallas_call(
        later_kernel,
        out_shape=jax.ShapeDtypeStruct(x.shape, x.dtype),
        in_specs=[ANY, ANY],
        out_specs=ANY,
        input_output_aliases={0: 0},
        compiler_params=params(4),
        name="later",
    )(x, after)


SCALE = math.log2(math.e) / math.sqrt(DH)


def scores_of(q, keys):
    return lax.dot_general(q, keys, (((1,), (1,)), ((), ())), preferred_element_type=F32)


def with_ones(values):
    return jnp.concatenate([values, jnp.ones(values.shape, BF)], axis=1)


def attend_kernel(place_ref, zero_ref, one_ref, two_ref, three_ref, own_ref, partner_ref, out_ref, q_ref):
    core, half, turned = place_ref[0], place_ref[2], place_ref[3]
    firsts = [half * HALF + i * DH for i in range(GH // 2)]
    for c in (core, 1 - core):
        for y in (turned, 1 - turned):
            firsts.append((1 - half) * HALF + (2 * c + y) * DH)
    for step, ref in enumerate((zero_ref, one_ref, two_ref, three_ref)):
        at = (place_ref[1] + 4 - step) % 4
        for head, first in enumerate(firsts):
            q_ref[at, head * TOK : (head + 1) * TOK, :] = ref[:, pl.ds(pl.multiple_of(first, DH), DH)]
    sides = [ref[...].reshape(4 * TOK, 2 * DH) for ref in (own_ref, partner_ref)]
    keys = [side[:, :DH] for side in sides]
    values = [with_ones(side[:, DH:]) for side in sides]
    heads = 4
    rows = heads * TOK
    own_row = lax.broadcasted_iota(jnp.int32, (rows, TOK), 0) & (TOK - 1)
    below = lax.broadcasted_iota(jnp.int32, (rows, TOK), 1) <= own_row
    shown = jnp.full((rows, TOK), half, jnp.int32) == 1
    for block in range(4):
        upto = (block + 1) * TOK
        before = upto - TOK
        key = jnp.concatenate([k[:upto] for k in keys], axis=0)
        value = jnp.concatenate([v[:upto] for v in values], axis=0)
        for head in range(0, GH, heads):
            q = q_ref[block, head * TOK : (head + heads) * TOK, :]
            score = scores_of(q, key)
            parts = []
            for side, seen in enumerate((below, shown)):
                if block:
                    parts.append(score[:, side * upto : side * upto + before])
                last = score[:, side * upto + before : (side + 1) * upto]
                parts.append(jnp.where(seen, last, -jnp.inf))
            score = jnp.concatenate(parts, axis=1)
            top = jnp.max(score, axis=1, keepdims=True)
            result = dot(jnp.exp2((score - top) * SCALE).astype(BF), value)
            result = (result[:, :DH] / result[:, DH:]).astype(BF)
            for i in range(heads):
                cols = slice((head + i) * DH, (head + i + 1) * DH)
                out_ref[block, :, cols] = result[i * TOK : (i + 1) * TOK]


def attend(place, blocks, own, partner):
    return pl.pallas_call(
        attend_kernel,
        out_shape=pltpu.VMEM((4, TOK, GH * DH), BF),
        in_specs=[SM] + [VM] * 6,
        out_specs=VM,
        scratch_shapes=[pltpu.VMEM((4, GH * TOK, DH), BF)],
        compiler_params=params(16),
        cost_estimate=pl.CostEstimate(
            flops=5 << 30, bytes_accessed=8 << 20, transcendentals=512 * 8 * 640
        ),
        name="attend",
    )(place, *(near_core(x) for x in (*blocks, own, partner)))


def project_kernel(steps, wanted, more, place_ref, heads_ref, mine_ref, *refs):
    others, added, out_refs = refs[:4], refs[4 : 4 + more], refs[4 + more :]
    rows = [heads_ref[(place_ref[1] + step) % 4] for step in steps]
    heads = rows[0] if len(rows) == 1 else jnp.concatenate(rows, axis=0)
    cols = 512
    for j in range(0, D, cols):
        span = slice(j, j + cols)
        weight = jnp.concatenate([mine_ref[:, span]] + [ref[:, span] for ref in others], axis=0)
        total = dot(heads, weight)
        for (i, low, high, kind), out_ref in zip(wanted, out_refs):
            if low <= j < high:
                out = total[i * TOK : (i + 1) * TOK]
                for ref in added:
                    out = out + ref[:, span].astype(F32)
                out_ref[:, j - low : j - low + cols] = out.astype(kind)


def project(steps, wanted, place, *arrays):
    return pl.pallas_call(
        functools.partial(project_kernel, steps, wanted, len(arrays) - 6),
        out_shape=[pltpu.VMEM((TOK, high - low), kind) for _, low, high, kind in wanted],
        in_specs=[SM] + [VM] * len(arrays),
        out_specs=[VM] * len(wanted),
        compiler_params=params(12),
        cost_estimate=pl.CostEstimate(
            flops=2 * len(steps) * TOK * 2 * HALF * D, bytes_accessed=8 << 20, transcendentals=0
        ),
        name="project",
    )(place, *(near_core(x) for x in arrays))


def join_kernel(a_ref, b_ref, c_ref, d_ref, left_ref, right_ref):
    left_ref[...] = (a_ref[...] + b_ref[...].astype(F32)).astype(BF)
    right_ref[...] = (c_ref[...] + d_ref[...].astype(F32)).astype(BF)


def join(*parts):
    return pl.pallas_call(
        join_kernel,
        out_shape=[pltpu.VMEM((TOK, D // 2), BF)] * 2,
        in_specs=[VM] * 4,
        out_specs=[VM] * 2,
        compiler_params=params(4),
        name="join",
    )(*(near_core(x) for x in parts))


def sum_over_z(hidden, *operands):
    half = D // 2
    left, right = project((2,), ((0, 0, half, BF), (0, half, D, BF)), *operands)
    left, right = turn(left, 1), turn(right, 3)
    wanted = ((0, half, D, BF), (1, 0, half, BF), (0, 0, half, F32), (1, half, D, F32))
    up_right, down_left, up_left, down_right = project((1, 3), wanted, *operands)
    up_right, down_left = turn(up_right, 1), turn(down_left, 3)
    (own,) = project((0,), ((0, 0, D, F32),), *operands, hidden)
    up_left, down_right = join(up_left, left, down_right, right)
    return own, turn(up_left, 1), up_right, down_left, turn(down_right, 3)


def residual_kernel(
    own_ref, up_left_ref, up_right_ref, down_left_ref, down_right_ref, gain_ref, pick1_ref, pick2_ref, att_ref, x_ref
):
    left = up_left_ref[...].astype(F32) + down_left_ref[...].astype(F32)
    right = up_right_ref[...].astype(F32) + down_right_ref[...].astype(F32)
    total = own_ref[...] + jnp.concatenate([left, right], axis=1)
    att_ref[...] = total.astype(BF)
    square = jnp.mean(total * total, axis=1, keepdims=True)
    normed = (total / jnp.sqrt(square + 1e-06) * gain_ref[...]).astype(BF)
    stack = jnp.concatenate([normed[:, : D // 2], normed[:, D // 2 :]], axis=0)
    rows = 256
    for first in range(0, NE * 8, rows):
        x_ref[first : first + rows, :D] = dot(pick1_ref[first : first + rows], normed).astype(BF)
        x_ref[first : first + rows, D:] = dot(pick2_ref[first : first + rows], stack).astype(BF)


def residual(sums, gain, pick1, pick2):
    return pl.pallas_call(
        residual_kernel,
        out_shape=(jax.ShapeDtypeStruct((TOK, D), BF), pltpu.VMEM((NE * 8, WIDE), BF)),
        in_specs=[VM] * 8,
        out_specs=(VM, VM),
        compiler_params=params(12),
        cost_estimate=pl.CostEstimate(flops=1 << 30, bytes_accessed=10 << 20, transcendentals=128),
        name="residual_norm_pick",
    )(*(near_core(x) for x in sums), gain.reshape(1, D), near_core(pick1), near_core(pick2))


def expert_kernel(x_ref, gate_ref, up_ref, down_ref, stat_ref, y_ref):
    rows = 512
    piece = 256
    count = piece // 2
    half = D // 2
    to = lax.broadcasted_iota(jnp.int32, (piece, piece), 0)
    at = lax.broadcasted_iota(jnp.int32, (piece, piece), 1)

    def source(i):
        side = (i >= count).astype(jnp.int32)
        own = i - side * count
        return (own >> 2) * 8 + side * 4 + (own & 3)

    sort = jnp.where(source(to) == at, 1.0, 0.0).astype(BF)
    back = jnp.where(source(at) == to, 1.0, 0.0).astype(BF)
    stat = jnp.broadcast_to(stat_ref[...][None], (rows // 8, 8, NE)).reshape(rows, NE).astype(BF)

    def step(i, carry):
        base = i * rows
        span = pl.ds(pl.multiple_of(base, rows), rows)
        pieces = [pl.ds(pl.multiple_of(base + p, piece), piece) for p in range(0, rows, piece)]
        parts = [x_ref[span, :D]]
        for at in pieces:
            rest = dot(sort, x_ref[at, D:]).astype(BF)
            parts.append(jnp.concatenate([rest[:count], rest[count:]], axis=1))
        x = jnp.concatenate(parts, axis=0)
        gate = dot(x, gate_ref[0])
        hidden = (gate / (1.0 + jnp.exp(-gate)) * dot(x, up_ref[0])).astype(BF)
        y = dot(hidden, down_ref[0]).astype(BF)
        y_ref[span, :D] = y[:rows]
        for p, at in enumerate(pieces):
            rest = y[rows + p * count : rows + (p + 1) * count]
            rest = jnp.concatenate([rest[:, :half], rest[:, half:]], axis=0)
            y_ref[at, D:WIDE] = dot(back, rest).astype(BF)
        y_ref[span, WIDE:] = stat
        return carry

    lax.fori_loop(0, NE * 8 // rows, step, 0)


def expert_apply(x, w_gate, w_up, w_down, stat):
    return pl.pallas_call(
        expert_kernel,
        out_shape=pltpu.VMEM((NE * 8, WIDE + NE), BF),
        in_specs=[VM] * 5,
        out_specs=VM,
        compiler_params=params(16),
        cost_estimate=pl.CostEstimate(
            flops=6 * NE * CAP * D * FF, bytes_accessed=22 << 20, transcendentals=NE * CAP * FF
        ),
        name="experts",
    )(near_core(x), near_core(w_gate), near_core(w_up), near_core(w_down), near_core(stat))


def mix_kernel(mix1_ref, mix2_ref, y_ref, out_ref, load_ref, loss_ref):
    cols = 512
    for j in range(D // cols):
        at = j * cols
        side = (j // 2) * 2 * TOK
        rest = D + (j % 2) * cols
        both = dot(mix1_ref[...], y_ref[:, at : at + cols])
        both = both + dot(mix2_ref[side : side + 2 * TOK], y_ref[:, rest : rest + cols])
        out_ref[:, at : at + cols] = (both[:TOK] + both[TOK:]).astype(BF)
    stat = jnp.sum(y_ref[:, WIDE:].astype(F32).reshape(NE, 8, NE), axis=0)
    counts = stat[0:1]
    gates = stat[1:2] + stat[2:3]
    tokens = TOK * NE
    load = counts / (tokens * TOP)
    load_ref[...] = NE * load
    loss = NE * jnp.sum(load * (gates / tokens), axis=1, keepdims=True)
    loss_ref[...] = jnp.broadcast_to(loss, (1, NE))


def mix(mix1, mix2, y):
    return pl.pallas_call(
        mix_kernel,
        out_shape=(
            jax.ShapeDtypeStruct((TOK, D), BF),
            jax.ShapeDtypeStruct((1, NE), F32),
            jax.ShapeDtypeStruct((1, NE), F32),
        ),
        in_specs=[VM] * 3,
        out_specs=(VM,) * 3,
        compiler_params=params(12),
        cost_estimate=pl.CostEstimate(flops=2 << 30, bytes_accessed=8 << 20, transcendentals=0),
        name="mix",
    )(near_core(mix1), near_core(mix2), near_core(y))


def swap(x, axis, count, step):
    return lax.ppermute(x, axis, [(i, i ^ step) for i in range(count)])


def turn(x, step):
    return lax.ppermute(x, "ctx", [(i, (i + 2 * step) % CTX) for i in range(CTX)])


def turn_all(blocks):
    return [blocks[0]] + [turn(blocks[step], step) for step in (1, 2, 3)]


def exchange(x):
    return lax.all_to_all(x, ALL, split_axis=0, concat_axis=0, tiled=True)


def on_device(
    hidden_in, queries, keys, values, out_weight, norm_gain, routes, gates, w_gate, w_up, w_down
):
    spot = lax.axis_index("ctx").astype(jnp.int32)
    column = lax.axis_index("dp").astype(jnp.int32)
    place = jnp.stack([column % 2, spot // 2, spot % 2, column // 2 % 2])
    *sent, weight = send_all(place, keys, values, queries, out_weight)
    first = lax.ppermute(weight, ALL, [(i, i ^ 65) for i in range(NE)])
    sent, blocks = turn_all(sent[:4]), turn_all(sent[4:])
    own = own_keys(place, sent, blocks[2])
    partner = swap(own, "ctx", CTX, 1)
    first = later(first, own)
    second = swap(first, "dp", 16, 2)
    first, second = later(first, partner), later(second, partner)
    third, fourth = swap(first, "dp", 16, 1), swap(second, "dp", 16, 1)
    pick1, pick2, mix1, mix2, stat = route_plan(routes, gates)
    heads = attend(place, blocks, own, partner)
    sums = sum_over_z(hidden_in, place, heads, out_weight, first, second, third, fourth)
    attended, x = residual(sums, norm_gain, pick1, pick2)
    x = exchange(x.reshape(NE, 8, WIDE))
    y = expert_apply(x.reshape(NE * 8, WIDE), w_gate, w_up, w_down, stat)
    y = exchange(y.reshape(NE, 8, WIDE + NE))
    expert_mix, load, loss = mix(mix1, mix2, y.reshape(NE * 8, WIDE + NE))
    return attended, expert_mix, loss[0, 0], load[0]


def solution(mesh):
    rows = P(ALL, None)
    return jax.shard_map(
        on_device,
        mesh=mesh,
        in_specs=(
            rows,
            rows,
            rows,
            rows,
            P("ctx", None),
            P(),
            rows,
            rows,
            P(ALL, None, None),
            P(ALL, None, None),
            P(ALL, None, None),
        ),
        out_specs=(rows, rows, P(), P()),
        check_vma=False,
    )
```

```python
import functools
import math

import jax
import jax.numpy as jnp
from jax import lax
from jax.experimental import pallas as pl
from jax.experimental.pallas import tpu as pltpu
from jax.sharding import PartitionSpec as P

H = 32
KV = 4
DH = 128
TOP = 8
D = 2048
FF = 768
TOK = 128
NE = 128
CTX = 8
GH = H // KV
HALF = 512
WHOLE = 8
CAP = 12
PIECE = 128
WIDE = 3072
ALL = ("dp", "ctx")
BF = jnp.bfloat16
F32 = jnp.float32
def params(megabytes):
    return pltpu.CompilerParams(vmem_limit_bytes=megabytes << 20)


def near_core(x):
    return pltpu.with_memory_space_constraint(x, pltpu.VMEM)


def far_memory(x):
    return pltpu.with_memory_space_constraint(x, pltpu.HBM)


ANY = pl.BlockSpec(memory_space=pl.ANY)
VM = pl.BlockSpec(memory_space=pltpu.VMEM)
SM = pl.BlockSpec(memory_space=pltpu.SMEM)


def dot(a, b):
    return jnp.dot(a, b, preferred_element_type=F32)


def route_kernel(routes_ref, gates_ref, pick1_ref, pick2_ref, mix1_ref, mix2_ref, stat_ref):
    experts = lax.broadcasted_iota(jnp.int32, (NE, TOK), 0)
    named = jnp.zeros((NE, TOK), F32)
    weight = jnp.zeros((NE, TOK), F32)
    for k in range(TOP):
        hit = routes_ref[k : k + 1, :] == experts
        named = jnp.where(hit, 1.0, named)
        weight = jnp.where(hit, gates_ref[k : k + 1, :], weight)
    earlier = lax.broadcasted_iota(jnp.int32, (TOK, TOK), 0) < lax.broadcasted_iota(
        jnp.int32, (TOK, TOK), 1
    )
    rank = dot(named.astype(BF), earlier.astype(F32).astype(BF))
    rank = jnp.where(named > 0, rank, -1.0)
    rank = jnp.broadcast_to(rank[:, None, :], (NE, 8, TOK)).reshape(NE * 8, TOK)
    weights = jnp.broadcast_to(weight[:, None, :], (NE, 8, TOK)).reshape(NE * 8, TOK)
    row = lax.broadcasted_iota(jnp.int32, (NE * 8, TOK), 0) & 7
    pick1 = rank == row.astype(F32)
    pick1_ref[...] = jnp.where(pick1, 1.0, 0.0).astype(BF)
    base = rank == (WHOLE + (row & 3)).astype(F32)
    left = base & (row < 4)
    right = base & (row >= 4)
    pick2_ref[:, :TOK] = jnp.where(left, 1.0, 0.0).astype(BF)
    pick2_ref[:, TOK:] = jnp.where(right, 1.0, 0.0).astype(BF)

    def put(ref, first, chosen):
        mix = jnp.transpose(jnp.where(chosen, weights, 0.0))
        ref[first : first + TOK, :] = mix.astype(BF)

    put(mix1_ref, 0, pick1)
    put(mix2_ref, 0, left)
    put(mix2_ref, TOK, right)
    stat_ref[...] = jnp.zeros((8, NE), F32)
    stat_ref[0:1, :] = jnp.sum(jnp.transpose(named), axis=0, keepdims=True)
    total = jnp.sum(jnp.transpose(weight), axis=0, keepdims=True)
    high = total.astype(BF).astype(F32)
    stat_ref[1:2, :] = high
    stat_ref[2:3, :] = total - high


def route_plan(routes, gates):
    return pl.pallas_call(
        route_kernel,
        out_shape=(
            pltpu.VMEM((NE * 8, TOK), BF),
            pltpu.VMEM((NE * 8, 2 * TOK), BF),
            pltpu.HBM((TOK, NE * 8), BF),
            pltpu.HBM((2 * TOK, NE * 8), BF),
            pltpu.HBM((8, NE), F32),
        ),
        in_specs=[VM] * 2,
        out_specs=(VM,) * 5,
        compiler_params=params(8),
        name="route_plan",
    )(routes.T, gates.T)


def fetch_all(pairs, sems):
    copies = [pltpu.make_async_copy(a, b, sems.at[i]) for i, (a, b) in enumerate(pairs)]
    for copy in copies:
        copy.start()
    for copy in copies:
        copy.wait()


def group_cols(place_ref, step, size):
    group = (place_ref[1] + step) % 4
    return pl.ds(pl.multiple_of(group * size, size), size)


def send_kernel(place_ref, keys_ref, values_ref, q_ref, weight_ref, *refs):
    rows = pl.ds(pl.multiple_of((2 * place_ref[0] + place_ref[3]) * PIECE, PIECE), PIECE)
    pairs = [(weight_ref.at[rows], refs[6])]
    wide = GH * DH
    for step, (kv_ref, base, query_ref) in enumerate(
        ((refs[0], 0, refs[3]), (refs[1], 0, refs[4]), (refs[5], wide, refs[5]), (refs[2], 0, refs[7]))
    ):
        cols = group_cols(place_ref, step, DH)
        pairs.append((keys_ref.at[:, cols], kv_ref.at[:, base : base + DH]))
        pairs.append((values_ref.at[:, cols], kv_ref.at[:, base + DH : base + 2 * DH]))
        pairs.append((q_ref.at[:, group_cols(place_ref, step, wide)], query_ref.at[:, :wide]))
    fetch_all(pairs, refs[8])


def send_all(place, *arrays):
    pair, block = pltpu.VMEM((TOK, 2 * DH), BF), pltpu.VMEM((TOK, GH * DH), BF)
    both = pltpu.VMEM((TOK, GH * DH + 2 * DH), BF)
    return pl.pallas_call(
        send_kernel,
        out_shape=[pair, pair, pair, block, block, both, pltpu.VMEM((PIECE, D), BF), block],
        in_specs=[SM] + [ANY] * 4,
        out_specs=[VM] * 8,
        scratch_shapes=[pltpu.SemaphoreType.DMA((13,))],
        compiler_params=params(4),
        name="send_all",
    )(place, *(far_memory(x) for x in arrays))


def own_keys_kernel(place_ref, *refs):
    for step in range(4):
        refs[4][(place_ref[1] + 4 - step) % 4] = refs[step][:, -2 * DH :]


def own_keys(place, blocks):
    return pl.pallas_call(
        own_keys_kernel,
        out_shape=pltpu.VMEM((4, TOK, 2 * DH), BF),
        in_specs=[SM] + [VM] * 4,
        out_specs=VM,
        compiler_params=params(4),
        name="own_keys",
    )(place, *(near_core(x) for x in blocks))


def later_kernel(x_ref, after_ref, out_ref):
    del x_ref, after_ref, out_ref


def later(x, after):
    return pl.pallas_call(
        later_kernel,
        out_shape=jax.ShapeDtypeStruct(x.shape, x.dtype),
        in_specs=[ANY, ANY],
        out_specs=ANY,
        input_output_aliases={0: 0},
        compiler_params=params(4),
        name="later",
    )(x, after)


def cut_kernel(x_ref, after_ref, top_ref, bottom_ref):
    del after_ref
    half = x_ref.shape[0] // 2
    top_ref[...] = x_ref[:half]
    bottom_ref[...] = x_ref[half:]


def cut(x, after):
    rows, cols = x.shape
    return pl.pallas_call(
        cut_kernel,
        out_shape=[pltpu.VMEM((rows // 2, cols), x.dtype)] * 2,
        in_specs=[VM, ANY],
        out_specs=[VM] * 2,
        compiler_params=params(4),
        name="cut",
    )(near_core(x), after)


def stack_kernel(top_ref, bottom_ref, after_ref, out_ref):
    del after_ref
    half = top_ref.shape[0]
    out_ref[:half] = top_ref[...]
    out_ref[half:] = bottom_ref[...]


def stack(top, bottom, after):
    rows, cols = top.shape
    return pl.pallas_call(
        stack_kernel,
        out_shape=pltpu.VMEM((2 * rows, cols), top.dtype),
        in_specs=[VM, VM, ANY],
        out_specs=VM,
        compiler_params=params(4),
        name="stack",
    )(near_core(top), near_core(bottom), after)


SCALE = math.log2(math.e) / math.sqrt(DH)


def scores_of(q, keys):
    return lax.dot_general(q, keys, (((1,), (1,)), ((), ())), preferred_element_type=F32)


def with_ones(values):
    return jnp.concatenate([values, jnp.ones(values.shape, BF)], axis=1)


def attend_kernel(place_ref, zero_ref, one_ref, two_ref, three_ref, own_ref, partner_ref, out_ref, q_ref):
    core, half, turned = place_ref[0], place_ref[2], place_ref[3]
    firsts = [half * HALF + i * DH for i in range(GH // 2)]
    for c in (core, 1 - core):
        for y in (turned, 1 - turned):
            firsts.append((1 - half) * HALF + (2 * c + y) * DH)
    for step, ref in enumerate((zero_ref, one_ref, two_ref, three_ref)):
        at = (place_ref[1] + 4 - step) % 4
        for head, first in enumerate(firsts):
            q_ref[at, head * TOK : (head + 1) * TOK, :] = ref[:, pl.ds(pl.multiple_of(first, DH), DH)]
    sides = [ref[...].reshape(4 * TOK, 2 * DH) for ref in (own_ref, partner_ref)]
    keys = [side[:, :DH] for side in sides]
    values = [with_ones(side[:, DH:]) for side in sides]
    heads = 4
    rows = heads * TOK
    own_row = lax.broadcasted_iota(jnp.int32, (rows, TOK), 0) & (TOK - 1)
    below = lax.broadcasted_iota(jnp.int32, (rows, TOK), 1) <= own_row
    shown = jnp.full((rows, TOK), half, jnp.int32) == 1
    for block in range(4):
        upto = (block + 1) * TOK
        before = upto - TOK
        key = jnp.concatenate([k[:upto] for k in keys], axis=0)
        value = jnp.concatenate([v[:upto] for v in values], axis=0)
        for head in range(0, GH, heads):
            q = q_ref[block, head * TOK : (head + heads) * TOK, :]
            score = scores_of(q, key)
            parts = []
            for side, seen in enumerate((below, shown)):
                if block:
                    parts.append(score[:, side * upto : side * upto + before])
                last = score[:, side * upto + before : (side + 1) * upto]
                parts.append(jnp.where(seen, last, -jnp.inf))
            score = jnp.concatenate(parts, axis=1)
            top = jnp.max(score, axis=1, keepdims=True)
            result = dot(jnp.exp2((score - top) * SCALE).astype(BF), value)
            result = (result[:, :DH] / result[:, DH:]).astype(BF)
            for i in range(heads):
                cols = slice((head + i) * DH, (head + i + 1) * DH)
                out_ref[block, :, cols] = result[i * TOK : (i + 1) * TOK]


def attend(place, blocks, own, partner):
    return pl.pallas_call(
        attend_kernel,
        out_shape=pltpu.VMEM((4, TOK, GH * DH), BF),
        in_specs=[SM] + [VM] * 6,
        out_specs=VM,
        scratch_shapes=[pltpu.VMEM((4, GH * TOK, DH), BF)],
        compiler_params=params(16),
        cost_estimate=pl.CostEstimate(
            flops=5 << 30, bytes_accessed=8 << 20, transcendentals=512 * 8 * 640
        ),
        name="attend",
    )(place, *(near_core(x) for x in (*blocks, own, partner)))


def project_kernel(steps, wanted, more, place_ref, heads_ref, mine_ref, *refs):
    others, added, out_refs = refs[:4], refs[4 : 4 + more], refs[4 + more :]
    rows = [heads_ref[(place_ref[1] + step) % 4] for step in steps]
    heads = rows[0] if len(rows) == 1 else jnp.concatenate(rows, axis=0)
    cols = 512
    for j in range(0, D, cols):
        span = slice(j, j + cols)
        weight = jnp.concatenate([mine_ref[:, span]] + [ref[:, span] for ref in others], axis=0)
        total = dot(heads, weight)
        for (i, low, high, kind), out_ref in zip(wanted, out_refs):
            if low <= j < high:
                out = total[i * TOK : (i + 1) * TOK]
                for ref in added:
                    out = out + ref[:, span].astype(F32)
                out_ref[:, j - low : j - low + cols] = out.astype(kind)


def project(steps, wanted, place, *arrays):
    return pl.pallas_call(
        functools.partial(project_kernel, steps, wanted, len(arrays) - 6),
        out_shape=[pltpu.VMEM((TOK, high - low), kind) for _, low, high, kind in wanted],
        in_specs=[SM] + [VM] * len(arrays),
        out_specs=[VM] * len(wanted),
        compiler_params=params(12),
        cost_estimate=pl.CostEstimate(
            flops=2 * len(steps) * TOK * 2 * HALF * D, bytes_accessed=8 << 20, transcendentals=0
        ),
        name="project",
    )(place, *(near_core(x) for x in arrays))


def join_kernel(a_ref, b_ref, c_ref, d_ref, left_ref, right_ref):
    left_ref[...] = (a_ref[...] + b_ref[...].astype(F32)).astype(BF)
    right_ref[...] = (c_ref[...] + d_ref[...].astype(F32)).astype(BF)


def join(*parts):
    return pl.pallas_call(
        join_kernel,
        out_shape=[pltpu.VMEM((TOK, D // 2), BF)] * 2,
        in_specs=[VM] * 4,
        out_specs=[VM] * 2,
        compiler_params=params(4),
        name="join",
    )(*(near_core(x) for x in parts))


def sum_over_z(hidden, *operands):
    half = D // 2
    left, right = project((2,), ((0, 0, half, BF), (0, half, D, BF)), *operands)
    left, right = turn(left, 1), turn(right, 3)
    wanted = ((0, half, D, BF), (1, 0, half, BF), (0, 0, half, F32), (1, half, D, F32))
    up_right, down_left, up_left, down_right = project((1, 3), wanted, *operands)
    up_right, down_left = turn(up_right, 1), turn(down_left, 3)
    (own,) = project((0,), ((0, 0, D, F32),), *operands, hidden)
    up_left, down_right = join(up_left, left, down_right, right)
    return own, turn(up_left, 1), up_right, down_left, turn(down_right, 3)


def residual_kernel(
    own_ref, up_left_ref, up_right_ref, down_left_ref, down_right_ref, gain_ref, pick1_ref, pick2_ref, att_ref, x_ref
):
    left = up_left_ref[...].astype(F32) + down_left_ref[...].astype(F32)
    right = up_right_ref[...].astype(F32) + down_right_ref[...].astype(F32)
    total = own_ref[...] + jnp.concatenate([left, right], axis=1)
    att_ref[...] = total.astype(BF)
    square = jnp.mean(total * total, axis=1, keepdims=True)
    normed = (total / jnp.sqrt(square + 1e-06) * gain_ref[...]).astype(BF)
    stack = jnp.concatenate([normed[:, : D // 2], normed[:, D // 2 :]], axis=0)
    rows = 256
    for first in range(0, NE * 8, rows):
        x_ref[first : first + rows, :D] = dot(pick1_ref[first : first + rows], normed).astype(BF)
        x_ref[first : first + rows, D:] = dot(pick2_ref[first : first + rows], stack).astype(BF)


def residual(sums, gain, pick1, pick2):
    return pl.pallas_call(
        residual_kernel,
        out_shape=(jax.ShapeDtypeStruct((TOK, D), BF), pltpu.VMEM((NE * 8, WIDE), BF)),
        in_specs=[VM] * 8,
        out_specs=(VM, VM),
        compiler_params=params(12),
        cost_estimate=pl.CostEstimate(flops=1 << 30, bytes_accessed=10 << 20, transcendentals=128),
        name="residual_norm_pick",
    )(*(near_core(x) for x in sums), gain.reshape(1, D), near_core(pick1), near_core(pick2))


def expert_kernel(x_ref, gate_ref, up_ref, down_ref, stat_ref, y_ref):
    rows = 512
    piece = 256
    count = piece // 2
    half = D // 2
    to = lax.broadcasted_iota(jnp.int32, (piece, piece), 0)
    at = lax.broadcasted_iota(jnp.int32, (piece, piece), 1)

    def source(i):
        side = (i >= count).astype(jnp.int32)
        own = i - side * count
        return (own >> 2) * 8 + side * 4 + (own & 3)

    sort = jnp.where(source(to) == at, 1.0, 0.0).astype(BF)
    back = jnp.where(source(at) == to, 1.0, 0.0).astype(BF)
    stat = jnp.broadcast_to(stat_ref[...][None], (rows // 8, 8, NE)).reshape(rows, NE).astype(BF)

    def step(i, carry):
        base = i * rows
        span = pl.ds(pl.multiple_of(base, rows), rows)
        pieces = [pl.ds(pl.multiple_of(base + p, piece), piece) for p in range(0, rows, piece)]
        parts = [x_ref[span, :D]]
        for at in pieces:
            rest = dot(sort, x_ref[at, D:]).astype(BF)
            parts.append(jnp.concatenate([rest[:count], rest[count:]], axis=1))
        x = jnp.concatenate(parts, axis=0)
        gate = dot(x, gate_ref[0])
        hidden = (gate / (1.0 + jnp.exp(-gate)) * dot(x, up_ref[0])).astype(BF)
        y = dot(hidden, down_ref[0]).astype(BF)
        y_ref[span, :D] = y[:rows]
        for p, at in enumerate(pieces):
            rest = y[rows + p * count : rows + (p + 1) * count]
            rest = jnp.concatenate([rest[:, :half], rest[:, half:]], axis=0)
            y_ref[at, D:WIDE] = dot(back, rest).astype(BF)
        y_ref[span, WIDE:] = stat
        return carry

    lax.fori_loop(0, NE * 8 // rows, step, 0)


def expert_apply(x, w_gate, w_up, w_down, stat):
    return pl.pallas_call(
        expert_kernel,
        out_shape=pltpu.VMEM((NE * 8, WIDE + NE), BF),
        in_specs=[VM] * 5,
        out_specs=VM,
        compiler_params=params(16),
        cost_estimate=pl.CostEstimate(
            flops=6 * NE * CAP * D * FF, bytes_accessed=22 << 20, transcendentals=NE * CAP * FF
        ),
        name="experts",
    )(near_core(x), near_core(w_gate), near_core(w_up), near_core(w_down), near_core(stat))


def mix_kernel(mix1_ref, mix2_ref, y_ref, out_ref, load_ref, loss_ref):
    cols = 512
    for j in range(D // cols):
        at = j * cols
        side = (j // 2) * TOK
        rest = D + (j % 2) * cols
        both = dot(mix1_ref[...], y_ref[:, at : at + cols])
        both = both + dot(mix2_ref[side : side + TOK], y_ref[:, rest : rest + cols])
        out_ref[:, at : at + cols] = both.astype(BF)
    stat = jnp.sum(y_ref[:, WIDE:].astype(F32).reshape(NE, 8, NE), axis=0)
    counts = stat[0:1]
    gates = stat[1:2] + stat[2:3]
    tokens = TOK * NE
    load = counts / (tokens * TOP)
    load_ref[...] = NE * load
    loss = NE * jnp.sum(load * (gates / tokens), axis=1, keepdims=True)
    loss_ref[...] = jnp.broadcast_to(loss, (1, NE))


def mix(mix1, mix2, y):
    return pl.pallas_call(
        mix_kernel,
        out_shape=(
            jax.ShapeDtypeStruct((TOK, D), BF),
            jax.ShapeDtypeStruct((1, NE), F32),
            jax.ShapeDtypeStruct((1, NE), F32),
        ),
        in_specs=[VM] * 3,
        out_specs=(VM,) * 3,
        compiler_params=params(12),
        cost_estimate=pl.CostEstimate(flops=2 << 30, bytes_accessed=8 << 20, transcendentals=0),
        name="mix",
    )(near_core(mix1), near_core(mix2), near_core(y))


def swap(x, axis, count, step):
    return lax.ppermute(x, axis, [(i, i ^ step) for i in range(count)])


def turn(x, step):
    return lax.ppermute(x, "ctx", [(i, (i + 2 * step) % CTX) for i in range(CTX)])


def along_y(x, step):
    return lax.ppermute(x, "dp", [(i, i // 8 * 8 + (i + 2 * step) % 8) for i in range(16)])


def exchange(x):
    return lax.all_to_all(x, ALL, split_axis=0, concat_axis=0, tiled=True)


def on_device(
    hidden_in, queries, keys, values, out_weight, norm_gain, routes, gates, w_gate, w_up, w_down
):
    spot = lax.axis_index("ctx").astype(jnp.int32)
    column = lax.axis_index("dp").astype(jnp.int32)
    place = jnp.stack([column % 2, spot // 2, spot % 2, column // 2 % 2])
    k0, k1, k3, q0, q1, both, weight, q3 = send_all(place, keys, values, queries, out_weight)
    first = lax.ppermute(weight, ALL, [(i, i ^ 65) for i in range(NE)])
    both = turn(both, 2)
    own = own_keys(place, (k0, turn(k1, 1), both, turn(k3, 3)))
    blocks = (q0, turn(q1, 1), both, turn(q3, 3))
    partner = swap(own, "ctx", CTX, 1)
    top, bottom = cut(first, own)
    second = stack(along_y(top, 1), along_y(bottom, 3), partner)
    first = later(first, partner)
    third, fourth = swap(first, "dp", 16, 1), swap(second, "dp", 16, 1)
    pick1, pick2, mix1, mix2, stat = route_plan(routes, gates)
    heads = attend(place, blocks, own, partner)
    sums = sum_over_z(hidden_in, place, heads, out_weight, first, second, third, fourth)
    attended, x = residual(sums, norm_gain, pick1, pick2)
    x = exchange(x.reshape(NE, 8, WIDE))
    y = expert_apply(x.reshape(NE * 8, WIDE), w_gate, w_up, w_down, stat)
    y = exchange(y.reshape(NE, 8, WIDE + NE))
    expert_mix, load, loss = mix(mix1, mix2, y.reshape(NE * 8, WIDE + NE))
    return attended, expert_mix, loss[0, 0], load[0]


def solution(mesh):
    rows = P(ALL, None)
    return jax.shard_map(
        on_device,
        mesh=mesh,
        in_specs=(
            rows,
            rows,
            rows,
            rows,
            P("ctx", None),
            P(),
            rows,
            rows,
            P(ALL, None, None),
            P(ALL, None, None),
            P(ALL, None, None),
        ),
        out_specs=(rows, rows, P(), P()),
        check_vma=False,
    )
```

```python
import functools
import math

import jax
import jax.numpy as jnp
from jax import lax
from jax.experimental import pallas as pl
from jax.experimental.pallas import tpu as pltpu
from jax.sharding import PartitionSpec as P

H = 32
KV = 4
DH = 128
TOP = 8
D = 2048
FF = 768
TOK = 128
NE = 128
CTX = 8
GH = H // KV
HALF = 512
WHOLE = 8
CAP = 12
PIECE = 128
WIDE = 3072
ALL = ("dp", "ctx")
BF = jnp.bfloat16
F32 = jnp.float32
def params(megabytes):
    return pltpu.CompilerParams(vmem_limit_bytes=megabytes << 20)


def near_core(x):
    return pltpu.with_memory_space_constraint(x, pltpu.VMEM)


def far_memory(x):
    return pltpu.with_memory_space_constraint(x, pltpu.HBM)


ANY = pl.BlockSpec(memory_space=pl.ANY)
VM = pl.BlockSpec(memory_space=pltpu.VMEM)
SM = pl.BlockSpec(memory_space=pltpu.SMEM)


def dot(a, b):
    return jnp.dot(a, b, preferred_element_type=F32)


def route_kernel(routes_ref, gates_ref, pick1_ref, pick2_ref, mix1_ref, mix2_ref, stat_ref):
    experts = lax.broadcasted_iota(jnp.int32, (NE, TOK), 0)
    named = jnp.zeros((NE, TOK), F32)
    weight = jnp.zeros((NE, TOK), F32)
    for k in range(TOP):
        hit = routes_ref[k : k + 1, :] == experts
        named = jnp.where(hit, 1.0, named)
        weight = jnp.where(hit, gates_ref[k : k + 1, :], weight)
    earlier = lax.broadcasted_iota(jnp.int32, (TOK, TOK), 0) < lax.broadcasted_iota(
        jnp.int32, (TOK, TOK), 1
    )
    rank = dot(named.astype(BF), earlier.astype(F32).astype(BF))
    rank = jnp.where(named > 0, rank, -1.0)
    rank = jnp.broadcast_to(rank[:, None, :], (NE, 8, TOK)).reshape(NE * 8, TOK)
    weights = jnp.broadcast_to(weight[:, None, :], (NE, 8, TOK)).reshape(NE * 8, TOK)
    row = lax.broadcasted_iota(jnp.int32, (NE * 8, TOK), 0) & 7
    pick1 = rank == row.astype(F32)
    pick1_ref[...] = jnp.where(pick1, 1.0, 0.0).astype(BF)
    base = rank == (WHOLE + (row & 3)).astype(F32)
    left = base & (row < 4)
    right = base & (row >= 4)
    pick2_ref[:, :TOK] = jnp.where(left, 1.0, 0.0).astype(BF)
    pick2_ref[:, TOK:] = jnp.where(right, 1.0, 0.0).astype(BF)

    def put(ref, first, chosen):
        mix = jnp.transpose(jnp.where(chosen, weights, 0.0))
        ref[first : first + TOK, :] = mix.astype(BF)

    put(mix1_ref, 0, pick1)
    put(mix2_ref, 0, left)
    put(mix2_ref, TOK, right)
    stat_ref[...] = jnp.zeros((8, NE), F32)
    stat_ref[0:1, :] = jnp.sum(jnp.transpose(named), axis=0, keepdims=True)
    total = jnp.sum(jnp.transpose(weight), axis=0, keepdims=True)
    high = total.astype(BF).astype(F32)
    stat_ref[1:2, :] = high
    stat_ref[2:3, :] = total - high


def route_plan(routes, gates):
    return pl.pallas_call(
        route_kernel,
        out_shape=(
            pltpu.VMEM((NE * 8, TOK), BF),
            pltpu.VMEM((NE * 8, 2 * TOK), BF),
            pltpu.HBM((TOK, NE * 8), BF),
            pltpu.HBM((2 * TOK, NE * 8), BF),
            pltpu.HBM((8, NE), F32),
        ),
        in_specs=[VM] * 2,
        out_specs=(VM,) * 5,
        compiler_params=params(8),
        name="route_plan",
    )(routes.T, gates.T)


def fetch_all(pairs, sems):
    copies = [pltpu.make_async_copy(a, b, sems.at[i]) for i, (a, b) in enumerate(pairs)]
    for copy in copies:
        copy.start()
    for copy in copies:
        copy.wait()


def group_cols(place_ref, step, size):
    group = (place_ref[1] + step) % 4
    return pl.ds(pl.multiple_of(group * size, size), size)


def send_kernel(place_ref, keys_ref, values_ref, q_ref, weight_ref, *refs):
    rows = pl.ds(pl.multiple_of((2 * place_ref[0] + place_ref[3]) * PIECE, PIECE), PIECE)
    pairs = [(weight_ref.at[rows], refs[6])]
    wide = GH * DH
    for step, (kv_ref, base, query_ref) in enumerate(
        ((refs[0], 0, refs[3]), (refs[1], 0, refs[4]), (refs[5], wide, refs[5]), (refs[2], 0, refs[7]))
    ):
        cols = group_cols(place_ref, step, DH)
        pairs.append((keys_ref.at[:, cols], kv_ref.at[:, base : base + DH]))
        pairs.append((values_ref.at[:, cols], kv_ref.at[:, base + DH : base + 2 * DH]))
        pairs.append((q_ref.at[:, group_cols(place_ref, step, wide)], query_ref.at[:, :wide]))
    fetch_all(pairs, refs[8])


def send_all(place, *arrays):
    pair, block = pltpu.VMEM((TOK, 2 * DH), BF), pltpu.VMEM((TOK, GH * DH), BF)
    both = pltpu.VMEM((TOK, GH * DH + 2 * DH), BF)
    return pl.pallas_call(
        send_kernel,
        out_shape=[pair, pair, pair, block, block, both, pltpu.VMEM((PIECE, D), BF), block],
        in_specs=[SM] + [ANY] * 4,
        out_specs=[VM] * 8,
        scratch_shapes=[pltpu.SemaphoreType.DMA((13,))],
        compiler_params=params(4),
        name="send_all",
    )(place, *(far_memory(x) for x in arrays))


def own_keys_kernel(place_ref, *refs):
    for step in range(4):
        refs[4][(place_ref[1] + 4 - step) % 4] = refs[step][:, -2 * DH :]


def own_keys(place, blocks):
    return pl.pallas_call(
        own_keys_kernel,
        out_shape=pltpu.VMEM((4, TOK, 2 * DH), BF),
        in_specs=[SM] + [VM] * 4,
        out_specs=VM,
        compiler_params=params(4),
        name="own_keys",
    )(place, *(near_core(x) for x in blocks))


def later_kernel(x_ref, after_ref, out_ref):
    del x_ref, after_ref, out_ref


def later(x, after):
    return pl.pallas_call(
        later_kernel,
        out_shape=jax.ShapeDtypeStruct(x.shape, x.dtype),
        in_specs=[ANY, ANY],
        out_specs=ANY,
        input_output_aliases={0: 0},
        compiler_params=params(4),
        name="later",
    )(x, after)


def cut_kernel(x_ref, after_ref, top_ref, bottom_ref):
    del after_ref
    half = x_ref.shape[0] // 2
    top_ref[...] = x_ref[:half]
    bottom_ref[...] = x_ref[half:]


def cut(x, after):
    rows, cols = x.shape
    return pl.pallas_call(
        cut_kernel,
        out_shape=[pltpu.VMEM((rows // 2, cols), x.dtype)] * 2,
        in_specs=[VM, ANY],
        out_specs=[VM] * 2,
        compiler_params=params(4),
        name="cut",
    )(near_core(x), after)


def stack_kernel(top_ref, bottom_ref, after_ref, out_ref):
    del after_ref
    half = top_ref.shape[0]
    out_ref[:half] = top_ref[...]
    out_ref[half:] = bottom_ref[...]


def stack(top, bottom, after):
    rows, cols = top.shape
    return pl.pallas_call(
        stack_kernel,
        out_shape=pltpu.VMEM((2 * rows, cols), top.dtype),
        in_specs=[VM, VM, ANY],
        out_specs=VM,
        compiler_params=params(4),
        name="stack",
    )(near_core(top), near_core(bottom), after)


SCALE = math.log2(math.e) / math.sqrt(DH)


def scores_of(q, keys):
    return lax.dot_general(q, keys, (((1,), (1,)), ((), ())), preferred_element_type=F32)


def with_ones(values):
    return jnp.concatenate([values, jnp.ones(values.shape, BF)], axis=1)


def attend_kernel(place_ref, zero_ref, one_ref, two_ref, three_ref, own_ref, partner_ref, out_ref, q_ref):
    core, half, turned = place_ref[0], place_ref[2], place_ref[3]
    firsts = [half * HALF + i * DH for i in range(GH // 2)]
    for c in (core, 1 - core):
        for y in (turned, 1 - turned):
            firsts.append((1 - half) * HALF + (2 * c + y) * DH)
    for step, ref in enumerate((zero_ref, one_ref, two_ref, three_ref)):
        at = (place_ref[1] + 4 - step) % 4
        for head, first in enumerate(firsts):
            q_ref[at, head * TOK : (head + 1) * TOK, :] = ref[:, pl.ds(pl.multiple_of(first, DH), DH)]
    sides = [ref[...].reshape(4 * TOK, 2 * DH) for ref in (own_ref, partner_ref)]
    keys = [side[:, :DH] for side in sides]
    values = [with_ones(side[:, DH:]) for side in sides]
    heads = 4
    rows = heads * TOK
    own_row = lax.broadcasted_iota(jnp.int32, (rows, TOK), 0) & (TOK - 1)
    below = lax.broadcasted_iota(jnp.int32, (rows, TOK), 1) <= own_row
    shown = jnp.full((rows, TOK), half, jnp.int32) == 1
    for block in range(4):
        upto = (block + 1) * TOK
        before = upto - TOK
        key = jnp.concatenate([k[:upto] for k in keys], axis=0)
        value = jnp.concatenate([v[:upto] for v in values], axis=0)
        for head in range(0, GH, heads):
            q = q_ref[block, head * TOK : (head + heads) * TOK, :]
            score = scores_of(q, key)
            parts = []
            for side, seen in enumerate((below, shown)):
                if block:
                    parts.append(score[:, side * upto : side * upto + before])
                last = score[:, side * upto + before : (side + 1) * upto]
                parts.append(jnp.where(seen, last, -jnp.inf))
            score = jnp.concatenate(parts, axis=1)
            top = jnp.max(score, axis=1, keepdims=True)
            result = dot(jnp.exp2((score - top) * SCALE).astype(BF), value)
            result = (result[:, :DH] / result[:, DH:]).astype(BF)
            for i in range(heads):
                cols = slice((head + i) * DH, (head + i + 1) * DH)
                out_ref[block, :, cols] = result[i * TOK : (i + 1) * TOK]


def attend(place, blocks, own, partner):
    return pl.pallas_call(
        attend_kernel,
        out_shape=pltpu.VMEM((4, TOK, GH * DH), BF),
        in_specs=[SM] + [VM] * 6,
        out_specs=VM,
        scratch_shapes=[pltpu.VMEM((4, GH * TOK, DH), BF)],
        compiler_params=params(16),
        cost_estimate=pl.CostEstimate(
            flops=5 << 30, bytes_accessed=8 << 20, transcendentals=512 * 8 * 640
        ),
        name="attend",
    )(place, *(near_core(x) for x in (*blocks, own, partner)))


def project_kernel(steps, wanted, more, place_ref, heads_ref, mine_ref, *refs):
    others, added, out_refs = refs[:4], refs[4 : 4 + more], refs[4 + more :]
    rows = [heads_ref[(place_ref[1] + step) % 4] for step in steps]
    heads = rows[0] if len(rows) == 1 else jnp.concatenate(rows, axis=0)
    cols = 512
    for j in range(0, D, cols):
        span = slice(j, j + cols)
        weight = jnp.concatenate([mine_ref[:, span]] + [ref[:, span] for ref in others], axis=0)
        total = dot(heads, weight)
        for (i, low, high, kind), out_ref in zip(wanted, out_refs):
            if low <= j < high:
                out = total[i * TOK : (i + 1) * TOK]
                for ref in added:
                    out = out + ref[:, span].astype(F32)
                out_ref[:, j - low : j - low + cols] = out.astype(kind)


def project(steps, wanted, place, *arrays):
    return pl.pallas_call(
        functools.partial(project_kernel, steps, wanted, len(arrays) - 6),
        out_shape=[pltpu.VMEM((TOK, high - low), kind) for _, low, high, kind in wanted],
        in_specs=[SM] + [VM] * len(arrays),
        out_specs=[VM] * len(wanted),
        compiler_params=params(12),
        cost_estimate=pl.CostEstimate(
            flops=2 * len(steps) * TOK * 2 * HALF * D, bytes_accessed=8 << 20, transcendentals=0
        ),
        name="project",
    )(place, *(near_core(x) for x in arrays))


def join_kernel(a_ref, b_ref, c_ref, d_ref, left_ref, right_ref):
    left_ref[...] = (a_ref[...] + b_ref[...].astype(F32)).astype(BF)
    right_ref[...] = (c_ref[...] + d_ref[...].astype(F32)).astype(BF)


def join(*parts):
    return pl.pallas_call(
        join_kernel,
        out_shape=[pltpu.VMEM((TOK, D // 2), BF)] * 2,
        in_specs=[VM] * 4,
        out_specs=[VM] * 2,
        compiler_params=params(4),
        name="join",
    )(*(near_core(x) for x in parts))


def sum_over_z(hidden, *operands):
    half = D // 2
    left, right = project((2,), ((0, 0, half, BF), (0, half, D, BF)), *operands)
    left, right = turn(left, 1), turn(right, 3)
    wanted = ((0, half, D, BF), (1, 0, half, BF), (0, 0, half, F32), (1, half, D, F32))
    up_right, down_left, up_left, down_right = project((1, 3), wanted, *operands)
    up_right, down_left = turn(up_right, 1), turn(down_left, 3)
    (own,) = project((0,), ((0, 0, D, F32),), *operands, hidden)
    up_left, down_right = join(up_left, left, down_right, right)
    return own, turn(up_left, 1), up_right, down_left, turn(down_right, 3)


def residual_kernel(
    own_ref, up_left_ref, up_right_ref, down_left_ref, down_right_ref, gain_ref, pick1_ref, pick2_ref, att_ref, x_ref
):
    left = up_left_ref[...].astype(F32) + down_left_ref[...].astype(F32)
    right = up_right_ref[...].astype(F32) + down_right_ref[...].astype(F32)
    total = own_ref[...] + jnp.concatenate([left, right], axis=1)
    att_ref[...] = total.astype(BF)
    square = jnp.mean(total * total, axis=1, keepdims=True)
    normed = (total / jnp.sqrt(square + 1e-06) * gain_ref[...]).astype(BF)
    stack = jnp.concatenate([normed[:, : D // 2], normed[:, D // 2 :]], axis=0)
    rows = 256
    for first in range(0, NE * 8, rows):
        x_ref[first : first + rows, :D] = dot(pick1_ref[first : first + rows], normed).astype(BF)
        x_ref[first : first + rows, D:] = dot(pick2_ref[first : first + rows], stack).astype(BF)


def residual(sums, gain, pick1, pick2):
    return pl.pallas_call(
        residual_kernel,
        out_shape=(jax.ShapeDtypeStruct((TOK, D), BF), pltpu.VMEM((NE * 8, WIDE), BF)),
        in_specs=[VM] * 8,
        out_specs=(VM, VM),
        compiler_params=params(12),
        cost_estimate=pl.CostEstimate(flops=1 << 30, bytes_accessed=10 << 20, transcendentals=128),
        name="residual_norm_pick",
    )(*(near_core(x) for x in sums), gain.reshape(1, D), near_core(pick1), near_core(pick2))


def expert_kernel(x_ref, gate_ref, up_ref, down_ref, stat_ref, y_ref):
    rows = 512
    piece = 256
    count = piece // 2
    half = D // 2
    to = lax.broadcasted_iota(jnp.int32, (piece, piece), 0)
    at = lax.broadcasted_iota(jnp.int32, (piece, piece), 1)

    def source(i):
        side = (i >= count).astype(jnp.int32)
        own = i - side * count
        return (own >> 2) * 8 + side * 4 + (own & 3)

    sort = jnp.where(source(to) == at, 1.0, 0.0).astype(BF)
    back = jnp.where(source(at) == to, 1.0, 0.0).astype(BF)
    stat = jnp.broadcast_to(stat_ref[...][None], (rows // 8, 8, NE)).reshape(rows, NE).astype(BF)

    def step(i, carry):
        base = i * rows
        span = pl.ds(pl.multiple_of(base, rows), rows)
        pieces = [pl.ds(pl.multiple_of(base + p, piece), piece) for p in range(0, rows, piece)]
        parts = [x_ref[span, :D]]
        for at in pieces:
            rest = dot(sort, x_ref[at, D:]).astype(BF)
            parts.append(jnp.concatenate([rest[:count], rest[count:]], axis=1))
        x = jnp.concatenate(parts, axis=0)
        gate = dot(x, gate_ref[0])
        hidden = (gate / (1.0 + jnp.exp(-gate)) * dot(x, up_ref[0])).astype(BF)
        y = dot(hidden, down_ref[0]).astype(BF)
        y_ref[span, :D] = y[:rows]
        for p, at in enumerate(pieces):
            rest = y[rows + p * count : rows + (p + 1) * count]
            rest = jnp.concatenate([rest[:, :half], rest[:, half:]], axis=0)
            y_ref[at, D:WIDE] = dot(back, rest).astype(BF)
        y_ref[span, WIDE:] = stat
        return carry

    lax.fori_loop(0, NE * 8 // rows, step, 0)


def expert_apply(x, w_gate, w_up, w_down, stat):
    return pl.pallas_call(
        expert_kernel,
        out_shape=pltpu.VMEM((NE * 8, WIDE + NE), BF),
        in_specs=[VM] * 5,
        out_specs=VM,
        compiler_params=params(16),
        cost_estimate=pl.CostEstimate(
            flops=6 * NE * CAP * D * FF, bytes_accessed=22 << 20, transcendentals=NE * CAP * FF
        ),
        name="experts",
    )(near_core(x), near_core(w_gate), near_core(w_up), near_core(w_down), near_core(stat))


def mix_kernel(mix1_ref, mix2_ref, y_ref, out_ref, load_ref, loss_ref):
    cols = 512
    for j in range(D // cols):
        at = j * cols
        side = (j // 2) * TOK
        rest = D + (j % 2) * cols
        both = dot(mix1_ref[...], y_ref[:, at : at + cols])
        both = both + dot(mix2_ref[side : side + TOK], y_ref[:, rest : rest + cols])
        out_ref[:, at : at + cols] = both.astype(BF)
    stat = jnp.sum(y_ref[:, WIDE:].astype(F32).reshape(NE, 8, NE), axis=0)
    counts = stat[0:1]
    gates = stat[1:2] + stat[2:3]
    tokens = TOK * NE
    load = counts / (tokens * TOP)
    load_ref[...] = NE * load
    loss = NE * jnp.sum(load * (gates / tokens), axis=1, keepdims=True)
    loss_ref[...] = jnp.broadcast_to(loss, (1, NE))


def mix(mix1, mix2, y):
    return pl.pallas_call(
        mix_kernel,
        out_shape=(
            jax.ShapeDtypeStruct((TOK, D), BF),
            jax.ShapeDtypeStruct((1, NE), F32),
            jax.ShapeDtypeStruct((1, NE), F32),
        ),
        in_specs=[VM] * 3,
        out_specs=(VM,) * 3,
        compiler_params=params(12),
        cost_estimate=pl.CostEstimate(flops=2 << 30, bytes_accessed=8 << 20, transcendentals=0),
        name="mix",
    )(near_core(mix1), near_core(mix2), near_core(y))


def swap(x, axis, count, step):
    return lax.ppermute(x, axis, [(i, i ^ step) for i in range(count)])


def turn(x, step):
    return lax.ppermute(x, "ctx", [(i, (i + 2 * step) % CTX) for i in range(CTX)])


def along_y(x, step):
    return lax.ppermute(x, "dp", [(i, i // 8 * 8 + (i + 2 * step) % 8) for i in range(16)])


def exchange(x):
    return lax.all_to_all(x, ALL, split_axis=0, concat_axis=0, tiled=True)


def on_device(
    hidden_in, queries, keys, values, out_weight, norm_gain, routes, gates, w_gate, w_up, w_down
):
    spot = lax.axis_index("ctx").astype(jnp.int32)
    column = lax.axis_index("dp").astype(jnp.int32)
    place = jnp.stack([column % 2, spot // 2, spot % 2, column // 2 % 2])
    k0, k1, k3, q0, q1, both, weight, q3 = send_all(place, keys, values, queries, out_weight)
    first = lax.ppermute(weight, ALL, [(i, i ^ 65) for i in range(NE)])
    both = turn(both, 2)
    own = own_keys(place, (k0, turn(k1, 1), both, turn(k3, 3)))
    blocks = (q0, turn(q1, 1), both, turn(q3, 3))
    partner = swap(own, "ctx", CTX, 1)
    top, bottom = cut(first, own)
    second = stack(along_y(top, 1), along_y(bottom, 3), blocks[1])
    first = later(first, blocks[3])
    third, fourth = swap(first, "dp", 16, 1), swap(second, "dp", 16, 1)
    pick1, pick2, mix1, mix2, stat = route_plan(routes, gates)
    heads = attend(place, blocks, own, partner)
    sums = sum_over_z(hidden_in, place, heads, out_weight, first, second, third, fourth)
    attended, x = residual(sums, norm_gain, pick1, pick2)
    x = exchange(x.reshape(NE, 8, WIDE))
    y = expert_apply(x.reshape(NE * 8, WIDE), w_gate, w_up, w_down, stat)
    y = exchange(y.reshape(NE, 8, WIDE + NE))
    expert_mix, load, loss = mix(mix1, mix2, y.reshape(NE * 8, WIDE + NE))
    return attended, expert_mix, loss[0, 0], load[0]


def solution(mesh):
    rows = P(ALL, None)
    return jax.shard_map(
        on_device,
        mesh=mesh,
        in_specs=(
            rows,
            rows,
            rows,
            rows,
            P("ctx", None),
            P(),
            rows,
            rows,
            P(ALL, None, None),
            P(ALL, None, None),
            P(ALL, None, None),
        ),
        out_specs=(rows, rows, P(), P()),
        check_vma=False,
    )
```

```python
import functools
import math

import jax
import jax.numpy as jnp
from jax import lax
from jax.experimental import pallas as pl
from jax.experimental.pallas import tpu as pltpu
from jax.sharding import PartitionSpec as P

H = 32
KV = 4
DH = 128
TOP = 8
D = 2048
FF = 768
TOK = 128
NE = 128
CTX = 8
GH = H // KV
HALF = 512
WHOLE = 8
CAP = 12
PIECE = 128
WIDE = 3072
ALL = ("dp", "ctx")
BF = jnp.bfloat16
F32 = jnp.float32
def params(megabytes):
    return pltpu.CompilerParams(vmem_limit_bytes=megabytes << 20)


def near_core(x):
    return pltpu.with_memory_space_constraint(x, pltpu.VMEM)


def far_memory(x):
    return pltpu.with_memory_space_constraint(x, pltpu.HBM)


ANY = pl.BlockSpec(memory_space=pl.ANY)
VM = pl.BlockSpec(memory_space=pltpu.VMEM)
SM = pl.BlockSpec(memory_space=pltpu.SMEM)


def dot(a, b):
    return jnp.dot(a, b, preferred_element_type=F32)


def route_kernel(routes_ref, gates_ref, pick1_ref, pick2_ref, mix1_ref, mix2_ref, stat_ref):
    experts = lax.broadcasted_iota(jnp.int32, (NE, TOK), 0)
    named = jnp.zeros((NE, TOK), F32)
    weight = jnp.zeros((NE, TOK), F32)
    for k in range(TOP):
        hit = routes_ref[k : k + 1, :] == experts
        named = jnp.where(hit, 1.0, named)
        weight = jnp.where(hit, gates_ref[k : k + 1, :], weight)
    earlier = lax.broadcasted_iota(jnp.int32, (TOK, TOK), 0) < lax.broadcasted_iota(
        jnp.int32, (TOK, TOK), 1
    )
    rank = dot(named.astype(BF), earlier.astype(F32).astype(BF))
    rank = jnp.where(named > 0, rank, -1.0)
    rank = jnp.broadcast_to(rank[:, None, :], (NE, 8, TOK)).reshape(NE * 8, TOK)
    weights = jnp.broadcast_to(weight[:, None, :], (NE, 8, TOK)).reshape(NE * 8, TOK)
    row = lax.broadcasted_iota(jnp.int32, (NE * 8, TOK), 0) & 7
    pick1 = rank == row.astype(F32)
    pick1_ref[...] = jnp.where(pick1, 1.0, 0.0).astype(BF)
    base = rank == (WHOLE + (row & 3)).astype(F32)
    left = base & (row < 4)
    right = base & (row >= 4)
    pick2_ref[:, :TOK] = jnp.where(left, 1.0, 0.0).astype(BF)
    pick2_ref[:, TOK:] = jnp.where(right, 1.0, 0.0).astype(BF)

    def put(ref, first, chosen):
        mix = jnp.transpose(jnp.where(chosen, weights, 0.0))
        ref[first : first + TOK, :] = mix.astype(BF)

    put(mix1_ref, 0, pick1)
    put(mix2_ref, 0, left)
    put(mix2_ref, TOK, right)
    stat_ref[...] = jnp.zeros((8, NE), F32)
    stat_ref[0:1, :] = jnp.sum(jnp.transpose(named), axis=0, keepdims=True)
    total = jnp.sum(jnp.transpose(weight), axis=0, keepdims=True)
    high = total.astype(BF).astype(F32)
    stat_ref[1:2, :] = high
    stat_ref[2:3, :] = total - high


def route_plan(routes, gates):
    return pl.pallas_call(
        route_kernel,
        out_shape=(
            pltpu.VMEM((NE * 8, TOK), BF),
            pltpu.VMEM((NE * 8, 2 * TOK), BF),
            pltpu.HBM((TOK, NE * 8), BF),
            pltpu.HBM((2 * TOK, NE * 8), BF),
            pltpu.HBM((8, NE), F32),
        ),
        in_specs=[VM] * 2,
        out_specs=(VM,) * 5,
        compiler_params=params(8),
        name="route_plan",
    )(routes.T, gates.T)


def fetch_all(pairs, sems):
    copies = [pltpu.make_async_copy(a, b, sems.at[i]) for i, (a, b) in enumerate(pairs)]
    for copy in copies:
        copy.start()
    for copy in copies:
        copy.wait()


def group_cols(place_ref, step, size):
    group = (place_ref[1] + step) % 4
    return pl.ds(pl.multiple_of(group * size, size), size)


def send_kernel(place_ref, keys_ref, values_ref, q_ref, weight_ref, *refs):
    rows = pl.ds(pl.multiple_of((2 * place_ref[0] + place_ref[3]) * PIECE, PIECE), PIECE)
    pairs = [(weight_ref.at[rows], refs[6])]
    wide = GH * DH
    for step, (kv_ref, base, query_ref) in enumerate(
        ((refs[0], 0, refs[3]), (refs[1], 0, refs[4]), (refs[5], wide, refs[5]), (refs[2], 0, refs[7]))
    ):
        cols = group_cols(place_ref, step, DH)
        pairs.append((keys_ref.at[:, cols], kv_ref.at[:, base : base + DH]))
        pairs.append((values_ref.at[:, cols], kv_ref.at[:, base + DH : base + 2 * DH]))
        pairs.append((q_ref.at[:, group_cols(place_ref, step, wide)], query_ref.at[:, :wide]))
    fetch_all(pairs, refs[8])


def send_all(place, *arrays):
    pair, block = pltpu.VMEM((TOK, 2 * DH), BF), pltpu.VMEM((TOK, GH * DH), BF)
    both = pltpu.VMEM((TOK, GH * DH + 2 * DH), BF)
    return pl.pallas_call(
        send_kernel,
        out_shape=[pair, pair, pair, block, block, both, pltpu.VMEM((PIECE, D), BF), block],
        in_specs=[SM] + [ANY] * 4,
        out_specs=[VM] * 8,
        scratch_shapes=[pltpu.SemaphoreType.DMA((13,))],
        compiler_params=params(4),
        name="send_all",
    )(place, *(far_memory(x) for x in arrays))


def own_keys_kernel(place_ref, *refs):
    for step in range(4):
        refs[4][(place_ref[1] + 4 - step) % 4] = refs[step][:, -2 * DH :]


def own_keys(place, blocks):
    return pl.pallas_call(
        own_keys_kernel,
        out_shape=pltpu.VMEM((4, TOK, 2 * DH), BF),
        in_specs=[SM] + [VM] * 4,
        out_specs=VM,
        compiler_params=params(4),
        name="own_keys",
    )(place, *(near_core(x) for x in blocks))


def later_kernel(x_ref, after_ref, out_ref):
    del x_ref, after_ref, out_ref


def later(x, after):
    return pl.pallas_call(
        later_kernel,
        out_shape=jax.ShapeDtypeStruct(x.shape, x.dtype),
        in_specs=[ANY, ANY],
        out_specs=ANY,
        input_output_aliases={0: 0},
        compiler_params=params(4),
        name="later",
    )(x, after)


def cut_kernel(x_ref, after_ref, top_ref, bottom_ref):
    del after_ref
    half = x_ref.shape[0] // 2
    top_ref[...] = x_ref[:half]
    bottom_ref[...] = x_ref[half:]


def cut(x, after):
    rows, cols = x.shape
    return pl.pallas_call(
        cut_kernel,
        out_shape=[pltpu.VMEM((rows // 2, cols), x.dtype)] * 2,
        in_specs=[VM, ANY],
        out_specs=[VM] * 2,
        compiler_params=params(4),
        name="cut",
    )(near_core(x), after)


def stack_kernel(top_ref, bottom_ref, after_ref, out_ref):
    del after_ref
    half = top_ref.shape[0]
    out_ref[:half] = top_ref[...]
    out_ref[half:] = bottom_ref[...]


def stack(top, bottom, after):
    rows, cols = top.shape
    return pl.pallas_call(
        stack_kernel,
        out_shape=pltpu.VMEM((2 * rows, cols), top.dtype),
        in_specs=[VM, VM, ANY],
        out_specs=VM,
        compiler_params=params(4),
        name="stack",
    )(near_core(top), near_core(bottom), after)


SCALE = math.log2(math.e) / math.sqrt(DH)


def scores_of(q, keys):
    return lax.dot_general(q, keys, (((1,), (1,)), ((), ())), preferred_element_type=F32)


def with_ones(values):
    return jnp.concatenate([values, jnp.ones(values.shape, BF)], axis=1)


def attend_kernel(place_ref, zero_ref, one_ref, two_ref, three_ref, own_ref, partner_ref, out_ref, q_ref):
    core, half, turned = place_ref[0], place_ref[2], place_ref[3]
    firsts = [half * HALF + i * DH for i in range(GH // 2)]
    for c in (core, 1 - core):
        for y in (turned, 1 - turned):
            firsts.append((1 - half) * HALF + (2 * c + y) * DH)
    for step, ref in enumerate((zero_ref, one_ref, two_ref, three_ref)):
        at = (place_ref[1] + 4 - step) % 4
        for head, first in enumerate(firsts):
            q_ref[at, head * TOK : (head + 1) * TOK, :] = ref[:, pl.ds(pl.multiple_of(first, DH), DH)]
    sides = [ref[...].reshape(4 * TOK, 2 * DH) for ref in (own_ref, partner_ref)]
    keys = [side[:, :DH] for side in sides]
    values = [with_ones(side[:, DH:]) for side in sides]
    heads = 4
    rows = heads * TOK
    own_row = lax.broadcasted_iota(jnp.int32, (rows, TOK), 0) & (TOK - 1)
    below = lax.broadcasted_iota(jnp.int32, (rows, TOK), 1) <= own_row
    shown = jnp.full((rows, TOK), half, jnp.int32) == 1
    for block in range(4):
        upto = (block + 1) * TOK
        before = upto - TOK
        key = jnp.concatenate([k[:upto] for k in keys], axis=0)
        value = jnp.concatenate([v[:upto] for v in values], axis=0)
        for head in range(0, GH, heads):
            q = q_ref[block, head * TOK : (head + heads) * TOK, :]
            score = scores_of(q, key)
            parts = []
            for side, seen in enumerate((below, shown)):
                if block:
                    parts.append(score[:, side * upto : side * upto + before])
                last = score[:, side * upto + before : (side + 1) * upto]
                parts.append(jnp.where(seen, last, -jnp.inf))
            score = jnp.concatenate(parts, axis=1)
            top = jnp.max(score, axis=1, keepdims=True)
            result = dot(jnp.exp2((score - top) * SCALE).astype(BF), value)
            result = (result[:, :DH] / result[:, DH:]).astype(BF)
            for i in range(heads):
                cols = slice((head + i) * DH, (head + i + 1) * DH)
                out_ref[block, :, cols] = result[i * TOK : (i + 1) * TOK]


def attend(place, blocks, own, partner):
    return pl.pallas_call(
        attend_kernel,
        out_shape=pltpu.VMEM((4, TOK, GH * DH), BF),
        in_specs=[SM] + [VM] * 6,
        out_specs=VM,
        scratch_shapes=[pltpu.VMEM((4, GH * TOK, DH), BF)],
        compiler_params=params(16),
        cost_estimate=pl.CostEstimate(
            flops=5 << 30, bytes_accessed=8 << 20, transcendentals=512 * 8 * 640
        ),
        name="attend",
    )(place, *(near_core(x) for x in (*blocks, own, partner)))


def project_kernel(steps, wanted, more, place_ref, heads_ref, mine_ref, *refs):
    others, added, out_refs = refs[:4], refs[4 : 4 + more], refs[4 + more :]
    rows = [heads_ref[(place_ref[1] + step) % 4] for step in steps]
    heads = rows[0] if len(rows) == 1 else jnp.concatenate(rows, axis=0)
    cols = 512
    for j in range(0, D, cols):
        span = slice(j, j + cols)
        weight = jnp.concatenate([mine_ref[:, span]] + [ref[:, span] for ref in others], axis=0)
        total = dot(heads, weight)
        for (i, low, high, kind), out_ref in zip(wanted, out_refs):
            if low <= j < high:
                out = total[i * TOK : (i + 1) * TOK]
                for ref in added:
                    out = out + ref[:, span].astype(F32)
                out_ref[:, j - low : j - low + cols] = out.astype(kind)


def project(steps, wanted, place, *arrays):
    return pl.pallas_call(
        functools.partial(project_kernel, steps, wanted, len(arrays) - 6),
        out_shape=[pltpu.VMEM((TOK, high - low), kind) for _, low, high, kind in wanted],
        in_specs=[SM] + [VM] * len(arrays),
        out_specs=[VM] * len(wanted),
        compiler_params=params(12),
        cost_estimate=pl.CostEstimate(
            flops=2 * len(steps) * TOK * 2 * HALF * D, bytes_accessed=8 << 20, transcendentals=0
        ),
        name="project",
    )(place, *(near_core(x) for x in arrays))


def join_kernel(a_ref, b_ref, c_ref, d_ref, left_ref, right_ref):
    left_ref[...] = (a_ref[...] + b_ref[...].astype(F32)).astype(BF)
    right_ref[...] = (c_ref[...] + d_ref[...].astype(F32)).astype(BF)


def join(*parts):
    return pl.pallas_call(
        join_kernel,
        out_shape=[pltpu.VMEM((TOK, D // 2), BF)] * 2,
        in_specs=[VM] * 4,
        out_specs=[VM] * 2,
        compiler_params=params(4),
        name="join",
    )(*(near_core(x) for x in parts))


def sum_over_z(hidden, *operands):
    half = D // 2
    left, right = project((2,), ((0, 0, half, BF), (0, half, D, BF)), *operands)
    left, right = turn(left, 1), turn(right, 3)
    wanted = ((0, half, D, BF), (1, 0, half, BF), (0, 0, half, F32), (1, half, D, F32))
    up_right, down_left, up_left, down_right = project((1, 3), wanted, *operands)
    up_right, down_left = turn(up_right, 1), turn(down_left, 3)
    (own,) = project((0,), ((0, 0, D, F32),), *operands, hidden)
    up_left, down_right = join(up_left, left, down_right, right)
    return own, turn(up_left, 1), up_right, down_left, turn(down_right, 3)


def residual_kernel(
    own_ref, up_left_ref, up_right_ref, down_left_ref, down_right_ref, gain_ref, pick1_ref, pick2_ref, att_ref, x_ref
):
    left = up_left_ref[...].astype(F32) + down_left_ref[...].astype(F32)
    right = up_right_ref[...].astype(F32) + down_right_ref[...].astype(F32)
    total = own_ref[...] + jnp.concatenate([left, right], axis=1)
    att_ref[...] = total.astype(BF)
    square = jnp.mean(total * total, axis=1, keepdims=True)
    normed = (total * (1.0 / jnp.sqrt(square + 1e-06)) * gain_ref[...]).astype(BF)
    stack = jnp.concatenate([normed[:, : D // 2], normed[:, D // 2 :]], axis=0)
    rows = 256
    for first in range(0, NE * 8, rows):
        x_ref[first : first + rows, :D] = dot(pick1_ref[first : first + rows], normed).astype(BF)
        x_ref[first : first + rows, D:] = dot(pick2_ref[first : first + rows], stack).astype(BF)


def residual(sums, gain, pick1, pick2):
    return pl.pallas_call(
        residual_kernel,
        out_shape=(jax.ShapeDtypeStruct((TOK, D), BF), pltpu.VMEM((NE * 8, WIDE), BF)),
        in_specs=[VM] * 8,
        out_specs=(VM, VM),
        compiler_params=params(12),
        cost_estimate=pl.CostEstimate(flops=1 << 30, bytes_accessed=10 << 20, transcendentals=128),
        name="residual_norm_pick",
    )(*(near_core(x) for x in sums), gain.reshape(1, D), near_core(pick1), near_core(pick2))


def expert_kernel(x_ref, gate_ref, up_ref, down_ref, stat_ref, y_ref):
    rows = 512
    piece = 256
    count = piece // 2
    half = D // 2
    to = lax.broadcasted_iota(jnp.int32, (piece, piece), 0)
    at = lax.broadcasted_iota(jnp.int32, (piece, piece), 1)

    def source(i):
        side = (i >= count).astype(jnp.int32)
        own = i - side * count
        return (own >> 2) * 8 + side * 4 + (own & 3)

    sort = jnp.where(source(to) == at, 1.0, 0.0).astype(BF)
    back = jnp.where(source(at) == to, 1.0, 0.0).astype(BF)
    stat = jnp.broadcast_to(stat_ref[...][None], (rows // 8, 8, NE)).reshape(rows, NE).astype(BF)

    def step(i, carry):
        base = i * rows
        span = pl.ds(pl.multiple_of(base, rows), rows)
        pieces = [pl.ds(pl.multiple_of(base + p, piece), piece) for p in range(0, rows, piece)]
        parts = [x_ref[span, :D]]
        for at in pieces:
            rest = dot(sort, x_ref[at, D:]).astype(BF)
            parts.append(jnp.concatenate([rest[:count], rest[count:]], axis=1))
        x = jnp.concatenate(parts, axis=0)
        gate = dot(x, gate_ref[0])
        hidden = (gate / (1.0 + jnp.exp(-gate)) * dot(x, up_ref[0])).astype(BF)
        y = dot(hidden, down_ref[0]).astype(BF)
        y_ref[span, :D] = y[:rows]
        for p, at in enumerate(pieces):
            rest = y[rows + p * count : rows + (p + 1) * count]
            rest = jnp.concatenate([rest[:, :half], rest[:, half:]], axis=0)
            y_ref[at, D:WIDE] = dot(back, rest).astype(BF)
        y_ref[span, WIDE:] = stat
        return carry

    lax.fori_loop(0, NE * 8 // rows, step, 0)


def expert_apply(x, w_gate, w_up, w_down, stat):
    return pl.pallas_call(
        expert_kernel,
        out_shape=pltpu.VMEM((NE * 8, WIDE + NE), BF),
        in_specs=[VM] * 5,
        out_specs=VM,
        compiler_params=params(16),
        cost_estimate=pl.CostEstimate(
            flops=6 * NE * CAP * D * FF, bytes_accessed=22 << 20, transcendentals=NE * CAP * FF
        ),
        name="experts",
    )(near_core(x), near_core(w_gate), near_core(w_up), near_core(w_down), near_core(stat))


def mix_kernel(mix1_ref, mix2_ref, y_ref, out_ref, load_ref, loss_ref):
    cols = 512
    for j in range(D // cols):
        at = j * cols
        side = (j // 2) * TOK
        rest = D + (j % 2) * cols
        both = dot(mix1_ref[...], y_ref[:, at : at + cols])
        both = both + dot(mix2_ref[side : side + TOK], y_ref[:, rest : rest + cols])
        out_ref[:, at : at + cols] = both.astype(BF)
    stat = jnp.sum(y_ref[:, WIDE:].astype(F32).reshape(NE, 8, NE), axis=0)
    counts = stat[0:1]
    gates = stat[1:2] + stat[2:3]
    tokens = TOK * NE
    load = counts / (tokens * TOP)
    load_ref[...] = NE * load
    loss = NE * jnp.sum(load * (gates / tokens), axis=1, keepdims=True)
    loss_ref[...] = jnp.broadcast_to(loss, (1, NE))


def mix(mix1, mix2, y):
    return pl.pallas_call(
        mix_kernel,
        out_shape=(
            jax.ShapeDtypeStruct((TOK, D), BF),
            jax.ShapeDtypeStruct((1, NE), F32),
            jax.ShapeDtypeStruct((1, NE), F32),
        ),
        in_specs=[VM] * 3,
        out_specs=(VM,) * 3,
        compiler_params=params(12),
        cost_estimate=pl.CostEstimate(flops=2 << 30, bytes_accessed=8 << 20, transcendentals=0),
        name="mix",
    )(near_core(mix1), near_core(mix2), near_core(y))


def swap(x, axis, count, step):
    return lax.ppermute(x, axis, [(i, i ^ step) for i in range(count)])


def turn(x, step):
    return lax.ppermute(x, "ctx", [(i, (i + 2 * step) % CTX) for i in range(CTX)])


def along_y(x, step):
    return lax.ppermute(x, "dp", [(i, i // 8 * 8 + (i + 2 * step) % 8) for i in range(16)])


def exchange(x):
    return lax.all_to_all(x, ALL, split_axis=0, concat_axis=0, tiled=True)


def on_device(
    hidden_in, queries, keys, values, out_weight, norm_gain, routes, gates, w_gate, w_up, w_down
):
    spot = lax.axis_index("ctx").astype(jnp.int32)
    column = lax.axis_index("dp").astype(jnp.int32)
    place = jnp.stack([column % 2, spot // 2, spot % 2, column // 2 % 2])
    k0, k1, k3, q0, q1, both, weight, q3 = send_all(place, keys, values, queries, out_weight)
    first = lax.ppermute(weight, ALL, [(i, i ^ 65) for i in range(NE)])
    both = turn(both, 2)
    own = own_keys(place, (k0, turn(k1, 1), both, turn(k3, 3)))
    blocks = (q0, turn(q1, 1), both, turn(q3, 3))
    partner = swap(own, "ctx", CTX, 1)
    top, bottom = cut(first, own)
    second = stack(along_y(top, 1), along_y(bottom, 3), blocks[1])
    first = later(first, blocks[3])
    third, fourth = swap(first, "dp", 16, 1), swap(second, "dp", 16, 1)
    pick1, pick2, mix1, mix2, stat = route_plan(routes, gates)
    heads = attend(place, blocks, own, partner)
    sums = sum_over_z(hidden_in, place, heads, out_weight, first, second, third, fourth)
    attended, x = residual(sums, norm_gain, pick1, pick2)
    x = exchange(x.reshape(NE, 8, WIDE))
    y = expert_apply(x.reshape(NE * 8, WIDE), w_gate, w_up, w_down, stat)
    y = exchange(y.reshape(NE, 8, WIDE + NE))
    expert_mix, load, loss = mix(mix1, mix2, y.reshape(NE * 8, WIDE + NE))
    return attended, expert_mix, loss[0, 0], load[0]


def solution(mesh):
    rows = P(ALL, None)
    return jax.shard_map(
        on_device,
        mesh=mesh,
        in_specs=(
            rows,
            rows,
            rows,
            rows,
            P("ctx", None),
            P(),
            rows,
            rows,
            P(ALL, None, None),
            P(ALL, None, None),
            P(ALL, None, None),
        ),
        out_specs=(rows, rows, P(), P()),
        check_vma=False,
    )
```
